128 devices in a mesh: dp: 8 (over z, core), expert: 16 (over y, x).
Axes of the slice: x: 4, y: 4, z: 4, core: 2. Of those that a mesh axis runs over, the one named last changes fastest.
Arguments:
- tokens: bfloat16 [25216, 768], P(('dp', 'expert')), may hold values from -6 to 6
- routes: int32 [25216, 2], P(('dp', 'expert')), may hold values from 0 to 15, all different within a row; in each aligned block of 197 rows (0 to 196, 197 to 393, ...) at most 31 rows name the same one
- cotangent: bfloat16 [25216, 768], P(('dp', 'expert')), may hold values from -6 to 6
- lead_norm_one: float32 [2, 768], P(None, ('dp', 'expert'))
- lead_norm_one_state: float32 [2, 2, 768], P(None, None, ('dp', 'expert')), as said below
- lead_mix: float32 [768, 2304], P(('dp', 'expert'))
- lead_mix_state: float32 [2, 768, 2304], P(None, ('dp', 'expert')), as said below
- lead_project: float32 [768, 768], P(('dp', 'expert')), may hold values from -0.875 to 0.875
- lead_project_state: float32 [2, 768, 768], P(None, ('dp', 'expert')), as said below
- lead_norm_two: float32 [2, 768], P(None, ('dp', 'expert'))
- lead_norm_two_state: float32 [2, 2, 768], P(None, None, ('dp', 'expert')), as said below
- lead_up: float32 [768, 3072], P('dp', 'expert'), may hold values from -0.21875 to 0.21875
- lead_up_state: float32 [2, 768, 3072], P(None, 'dp', 'expert'), as said below
- lead_down: float32 [3072, 768], P('expert', 'dp'), may hold values from -0.109375 to 0.109375
- lead_down_state: float32 [2, 3072, 768], P(None, 'expert', 'dp'), as said below
- norm_first: float32 [2, 768], P(None, ('dp', 'expert'))
- norm_first_state: float32 [2, 2, 768], P(None, None, ('dp', 'expert')), as said below
- mix_weight: float32 [768, 2304], P(('dp', 'expert'))
- mix_state: float32 [2, 768, 2304], P(None, ('dp', 'expert')), as said below
- project_weight: float32 [768, 768], P(('dp', 'expert')), may hold values from -0.875 to 0.875
- project_state: float32 [2, 768, 768], P(None, ('dp', 'expert')), as said below
- norm_second: float32 [2, 768], P(None, ('dp', 'expert'))
- norm_second_state: float32 [2, 2, 768], P(None, None, ('dp', 'expert')), as said below
- router_weight: float32 [768, 16], P(('dp', 'expert')), may hold values from -0.21875 to 0.21875
- router_state: float32 [2, 768, 16], P(None, ('dp', 'expert')), as said below
- expert_in: float32 [16, 768, 3072], P('expert', None, 'dp'), may hold values from -0.21875 to 0.21875
- expert_in_state: float32 [2, 16, 768, 3072], P(None, 'expert', None, 'dp'), as said below
- expert_out: float32 [16, 3072, 768], P('expert', 'dp'), may hold values from -0.109375 to 0.109375
- expert_out_state: float32 [2, 16, 3072, 768], P(None, 'expert', 'dp'), as said below
Outputs:
- block_out: bfloat16 [25216, 768], P(('dp', 'expert'))
- token_input_grad: float32 [25216, 768], P(('dp', 'expert'))
- lead_norm_one_grad: float32 [2, 768], P(None, ('dp', 'expert'))
- lead_norm_one_new: float32 [2, 768], P(None, ('dp', 'expert'))
- lead_norm_one_state_new: float32 [2, 2, 768], P(None, None, ('dp', 'expert'))
- lead_mix_grad: float32 [768, 2304], P(('dp', 'expert'))
- lead_mix_new: float32 [768, 2304], P(('dp', 'expert'))
- lead_mix_state_new: float32 [2, 768, 2304], P(None, ('dp', 'expert'))
- lead_project_grad: float32 [768, 768], P(('dp', 'expert'))
- lead_project_new: float32 [768, 768], P(('dp', 'expert'))
- lead_project_state_new: float32 [2, 768, 768], P(None, ('dp', 'expert'))
- leading_second_norm_grad: float32 [2, 768], P(None, ('dp', 'expert'))
- lead_norm_two_new: float32 [2, 768], P(None, ('dp', 'expert'))
- lead_norm_two_state_new: float32 [2, 2, 768], P(None, None, ('dp', 'expert'))
- lead_up_grad: float32 [768, 3072], P('dp', 'expert')
- lead_up_new: float32 [768, 3072], P('dp', 'expert')
- lead_up_state_new: float32 [2, 768, 3072], P(None, 'dp', 'expert')
- lead_down_grad: float32 [3072, 768], P('expert', 'dp')
- lead_down_new: float32 [3072, 768], P('expert', 'dp')
- lead_down_state_new: float32 [2, 3072, 768], P(None, 'expert', 'dp')
- norm_first_grad: float32 [2, 768], P(None, ('dp', 'expert'))
- norm_first_new: float32 [2, 768], P(None, ('dp', 'expert'))
- norm_first_state_new: float32 [2, 2, 768], P(None, None, ('dp', 'expert'))
- mix_grad: float32 [768, 2304], P(('dp', 'expert'))
- mix_new: float32 [768, 2304], P(('dp', 'expert'))
- mix_state_new: float32 [2, 768, 2304], P(None, ('dp', 'expert'))
- project_grad: float32 [768, 768], P(('dp', 'expert'))
- project_new: float32 [768, 768], P(('dp', 'expert'))
- project_state_new: float32 [2, 768, 768], P(None, ('dp', 'expert'))
- second_norm_param_grad: float32 [2, 768], P(None, ('dp', 'expert'))
- norm_second_new: float32 [2, 768], P(None, ('dp', 'expert'))
- norm_second_state_new: float32 [2, 2, 768], P(None, None, ('dp', 'expert'))
- router_grad: float32 [768, 16], P(('dp', 'expert'))
- router_new: float32 [768, 16], P(('dp', 'expert'))
- router_state_new: float32 [2, 768, 16], P(None, ('dp', 'expert'))
- expert_in_grad: float32 [16, 768, 3072], P('expert', None, 'dp')
- expert_in_new: float32 [16, 768, 3072], P('expert', None, 'dp')
- expert_in_state_new: float32 [2, 16, 768, 3072], P(None, 'expert', None, 'dp')
- expert_out_grad: float32 [16, 3072, 768], P('expert', 'dp')
- expert_out_new: float32 [16, 3072, 768], P('expert', 'dp')
- expert_out_state_new: float32 [2, 16, 3072, 768], P(None, 'expert', 'dp')
The draws below stay inside these ranges and needn't reach their ends.
Inputs may be any that keep to these rules, and one draw needn't show every extreme that they name: `routes`: in the rows of one device no expert is named more than 31 times. `lead_norm_one_state`: second moments are positive. `lead_mix_state`: second moments are positive. `lead_project_state`: second moments are positive. `lead_norm_two_state`: second moments are positive. `lead_up_state`: second moments are positive. `lead_down_state`: second moments are positive. `norm_first_state`: second moments are positive. `mix_state`: second moments are positive. `project_state`: second moments are positive. `norm_second_state`: second moments are positive. `router_state`: second moments are positive. `expert_in_state`: second moments are positive. `expert_out_state`: second moments are positive.
All inputs are finite; a program needn't handle non-finite values.
Results may differ from the reference program's by a relative error of at most 0.023.
Values may be sent and summed in bfloat16 or wider, within the bound.
A program may use at most 192 MiB of HBM per device.

```python
import math
import jax
import jax.numpy as jnp
import numpy as np
from jax import lax

D = 768
HEADS = 12
HEAD_DIM = 64
HID = 3072
SEQ = 197
STEP = 3
TOK_DEV = 197
TOKENS = 25216
EXPERTS = 16
CAP = 31
DEVICES = 128


def state_pair(key, shape, grad_scale):
    first = 0.1 * grad_scale * jax.random.normal(jax.random.fold_in(key, 11), shape, jnp.float32)
    spread = jnp.exp(jax.random.uniform(jax.random.fold_in(key, 12), shape, jnp.float32, -math.log(2.0), math.log(2.0)))
    second = 0.001 / 0.999 * 2.0 * grad_scale * grad_scale * spread
    return jnp.stack([first, second])


def norm_pair(key):
    norm_gain = jax.random.uniform(jax.random.fold_in(key, 1), (D,), jnp.float32, 0.6, 1.4)
    norm_shift = 0.3 * jax.random.normal(jax.random.fold_in(key, 2), (D,), jnp.float32)
    return jnp.stack([norm_gain, norm_shift])


def mix_draw(key):
    return D ** (-0.5) * jax.random.normal(key, (D, 3 * D), jnp.float32)


def draw_lead_norm_one(key, part):
    return norm_pair(jax.random.fold_in(key, 101))


def draw_lead_norm_two(key, part):
    return norm_pair(jax.random.fold_in(key, 102))


def draw_norm_first(key, part):
    return norm_pair(jax.random.fold_in(key, 103))


def draw_norm_second(key, part):
    return norm_pair(jax.random.fold_in(key, 104))


def draw_lead_mix(key, part):
    return mix_draw(jax.random.fold_in(key, 201))


def draw_mix_weight(key, part):
    return mix_draw(jax.random.fold_in(key, 202))


def draw_lead_norm_one_state(key, part):
    return state_pair(jax.random.fold_in(key, 301), (2, D), 1.2 * math.sqrt(TOKENS))


def draw_lead_mix_state(key, part):
    return state_pair(jax.random.fold_in(key, 302), (D, 3 * D), 0.7 * math.sqrt(TOKENS))


def draw_lead_project_state(key, part):
    return state_pair(jax.random.fold_in(key, 303), (D, D), 0.12 * math.sqrt(TOKENS))


def draw_lead_norm_two_state(key, part):
    return state_pair(jax.random.fold_in(key, 304), (2, D), 0.5 * math.sqrt(TOKENS))


def draw_lead_up_state(key, part):
    return state_pair(jax.random.fold_in(key, 305), (D, HID), 0.35 * math.sqrt(TOKENS))


def draw_lead_down_state(key, part):
    return state_pair(jax.random.fold_in(key, 306), (HID, D), 0.5 * math.sqrt(TOKENS))


def draw_norm_first_state(key, part):
    return state_pair(jax.random.fold_in(key, 307), (2, D), 1.2 * math.sqrt(TOKENS))


def draw_mix_state(key, part):
    return state_pair(jax.random.fold_in(key, 308), (D, 3 * D), 0.7 * math.sqrt(TOKENS))


def draw_project_state(key, part):
    return state_pair(jax.random.fold_in(key, 309), (D, D), 0.12 * math.sqrt(TOKENS))


def draw_norm_second_state(key, part):
    return state_pair(jax.random.fold_in(key, 310), (2, D), 0.5 * math.sqrt(TOKENS))


def draw_router_state(key, part):
    return state_pair(jax.random.fold_in(key, 311), (D, EXPERTS), 5.0 * math.sqrt(2.0 * TOKENS / EXPERTS))


def draw_expert_in_state(key, part):
    return state_pair(jax.random.fold_in(key, 312), (EXPERTS, D, HID), 0.17 * math.sqrt(2.0 * TOKENS / EXPERTS))


def draw_expert_out_state(key, part):
    return state_pair(jax.random.fold_in(key, 313), (EXPERTS, HID, D), 0.36 * math.sqrt(2.0 * TOKENS / EXPERTS))


def block_scale(key, extent, cuts, low, high):
    def one(axis_at, blocks):
        steps = jax.random.uniform(jax.random.fold_in(jax.random.fold_in(key, 6), axis_at), (blocks,), jnp.float32, low / len(cuts), high / len(cuts))
        return jnp.repeat(jnp.exp(steps), extent[axis_at] // blocks).reshape((-1,) + (1,) * (len(extent) - axis_at - 1))

    level = one(*cuts[0])
    for cut in cuts[1:]:
        level = level * one(*cut)
    return level


def shared_out(own_key, own, number, rows, amount, top, limit, slope):
    order = jax.random.permutation(own_key, amount)
    crowded, common = portions_of(amount, rows * top, limit, slope, True), portions_of(amount, rows * top, limit, slope, False)
    places = jnp.arange(amount)

    def named(tallies, turn):
        used = int((tallies > 0).sum())
        fixed = max(1, used // 4)
        moved = fixed + (places - fixed + turn * (used - fixed)) % max(1, amount - fixed)
        return jnp.zeros((amount,), jnp.int32).at[order[jnp.where(places < fixed, places, moved)]].set(jnp.asarray(tallies, jnp.int32))

    tallies = jnp.where(number % 4 == 0, named(crowded, number // 4), named(common, number - number // 4 - 1))
    mixed = jax.random.permutation(jax.random.fold_in(own, 3), amount)
    donor, sink = mixed[0:amount // 2 * 2:2], mixed[1:amount // 2 * 2:2]
    slack = jnp.minimum(tallies[donor] - 1, limit - tallies[sink]) // 2
    slack = jnp.where((donor == order[0]) | (sink == order[0]) | (tallies[sink] == 0), 0, jnp.maximum(slack, 0))
    moved = jax.random.randint(jax.random.fold_in(own, 4), (amount // 2,), 0, 1 << 20) % (slack + 1)
    tallies = tallies.at[donor].add(-moved).at[sink].add(moved)
    members = jnp.searchsorted(jnp.cumsum(tallies), jnp.arange(rows * top), side="right").astype(jnp.int32)
    listing = members.reshape(top, rows).T
    listing = listing[jax.random.permutation(jax.random.fold_in(own, 1), rows)]
    turn = jax.random.randint(jax.random.fold_in(own, 2), (rows, 1), 0, top)
    return jnp.take_along_axis(listing, (jnp.arange(top)[None, :] + turn) % top, axis=1)


def portions_of(count, total, most, slope, full):
    loads = [(1 << 20) // math.isqrt(standing ** slope) + 1 for standing in range(1, count + 1)]
    largest = most if full else min(most, max(-(-total // count), total * loads[0] // sum(loads)))
    least = 1 if total - largest >= count - 1 else 0
    counts, rest = [largest] + [least] * (count - 1), total - largest - least * (count - 1)
    while rest > 0:
        movable = [i for i in range(1, count) if counts[i] < largest] or [i for i in range(1, count) if counts[i] < most]
        whole, budget = sum([loads[i] for i in movable]), rest
        for i in movable:
            addition = min(most - counts[i], max(1, budget * loads[i] // whole), rest)
            counts[i] = counts[i] + addition
            rest = rest - addition
    return np.array(counts)


def scatter_about(rng, extent, scale, limit, pieces=(), kind=jnp.bfloat16):
    values = scale * jax.random.normal(rng, extent, jnp.float32)
    if pieces:
        values = values * block_scale(rng, extent, pieces, -0.22, 0.18)
    return jnp.clip(values, -limit, limit).astype(kind)


def setup_inputs(seed: int = 0) -> dict:
    key_of = jax.random.split(jax.random.key(seed), 30)
    tokens = scatter_about(key_of[0], (TOKENS, D), 1.0, 6.0, ((0, 128),))
    routes_keys = jax.random.split(jax.random.fold_in(key_of[1], 1), TOKENS // TOK_DEV)
    routes_turns = jax.random.permutation(jax.random.fold_in(key_of[1], 3), TOKENS // TOK_DEV)
    routes = jax.vmap(lambda own, number: shared_out(jax.random.fold_in(key_of[1], 2), own, number, TOK_DEV, EXPERTS, 2, CAP, 1))(routes_keys, routes_turns).reshape((TOKENS, 2))
    cotangent = scatter_about(key_of[2], (TOKENS, D), 1.0, 6.0, ((0, 128),))
    lead_norm_one = draw_lead_norm_one(jax.random.fold_in(key_of[29], 71), 0)
    lead_norm_one_state = draw_lead_norm_one_state(jax.random.fold_in(key_of[29], 71), 0)
    lead_mix = draw_lead_mix(jax.random.fold_in(key_of[29], 71), 0)
    lead_mix_state = draw_lead_mix_state(jax.random.fold_in(key_of[29], 71), 0)
    lead_project = scatter_about(key_of[7], (D, D), (D // 16) ** -0.5, 0.875, ((0, 128),), jnp.float32)
    lead_project_state = draw_lead_project_state(jax.random.fold_in(key_of[29], 71), 0)
    lead_norm_two = draw_lead_norm_two(jax.random.fold_in(key_of[29], 71), 0)
    lead_norm_two_state = draw_lead_norm_two_state(jax.random.fold_in(key_of[29], 71), 0)
    lead_up = scatter_about(key_of[11], (D, HID), D ** -0.5, 0.21875, ((0, 8), (1, 16)), jnp.float32)
    lead_up_state = draw_lead_up_state(jax.random.fold_in(key_of[29], 71), 0)
    lead_down = scatter_about(key_of[13], (HID, D), HID ** -0.5, 0.109375, ((0, 16), (1, 8)), jnp.float32)
    lead_down_state = draw_lead_down_state(jax.random.fold_in(key_of[29], 71), 0)
    norm_first = draw_norm_first(jax.random.fold_in(key_of[29], 71), 0)
    norm_first_state = draw_norm_first_state(jax.random.fold_in(key_of[29], 71), 0)
    mix_weight = draw_mix_weight(jax.random.fold_in(key_of[29], 71), 0)
    mix_state = draw_mix_state(jax.random.fold_in(key_of[29], 71), 0)
    project_weight = scatter_about(key_of[19], (D, D), (D // 16) ** -0.5, 0.875, ((0, 128),), jnp.float32)
    project_state = draw_project_state(jax.random.fold_in(key_of[29], 71), 0)
    norm_second = draw_norm_second(jax.random.fold_in(key_of[29], 71), 0)
    norm_second_state = draw_norm_second_state(jax.random.fold_in(key_of[29], 71), 0)
    router_weight = scatter_about(key_of[23], (D, EXPERTS), D ** -0.5, 0.21875, ((0, 128),), jnp.float32)
    router_state = draw_router_state(jax.random.fold_in(key_of[29], 71), 0)
    expert_in = scatter_about(key_of[25], (EXPERTS, D, HID), D ** -0.5, 0.21875, ((0, 16), (2, 8)), jnp.float32)
    expert_in_state = draw_expert_in_state(jax.random.fold_in(key_of[29], 71), 0)
    expert_out = scatter_about(key_of[27], (EXPERTS, HID, D), HID ** -0.5, 0.109375, ((0, 16), (1, 8)), jnp.float32)
    expert_out_state = draw_expert_out_state(jax.random.fold_in(key_of[29], 71), 0)
    return dict(tokens=tokens, routes=routes, cotangent=cotangent, lead_norm_one=lead_norm_one, lead_norm_one_state=lead_norm_one_state, lead_mix=lead_mix, lead_mix_state=lead_mix_state, lead_project=lead_project, lead_project_state=lead_project_state, lead_norm_two=lead_norm_two, lead_norm_two_state=lead_norm_two_state, lead_up=lead_up, lead_up_state=lead_up_state, lead_down=lead_down, lead_down_state=lead_down_state, norm_first=norm_first, norm_first_state=norm_first_state, mix_weight=mix_weight, mix_state=mix_state, project_weight=project_weight, project_state=project_state, norm_second=norm_second, norm_second_state=norm_second_state, router_weight=router_weight, router_state=router_state, expert_in=expert_in, expert_in_state=expert_in_state, expert_out=expert_out, expert_out_state=expert_out_state)


norm_eps = 1e-06
beta_one = 0.9
beta_two = 0.999
adam_eps = 1e-08
matrix_rate = 0.03
norm_rate = 0.3
decay_rate = 0.05
root_half = 0.7071067811865476
inv_root_tau = 0.3989422804014327

def layer_normalize(rows):
    center = lax.optimization_barrier(jnp.mean(rows, axis=-1, keepdims=True))
    offset = rows - center
    spread = lax.optimization_barrier(jnp.mean(offset * offset, axis=-1, keepdims=True))
    inverse_stddev = lax.rsqrt(spread + norm_eps)
    return (offset * inverse_stddev, inverse_stddev)

def norm_backward_pass(upper_bound, centered_scaled, inverse_stddev, norm_gain):
    scaled_rows = upper_bound * norm_gain
    return inverse_stddev * (scaled_rows - lax.optimization_barrier(jnp.mean(scaled_rows, axis=-1, keepdims=True)) - centered_scaled * lax.optimization_barrier(jnp.mean(scaled_rows * centered_scaled, axis=-1, keepdims=True)))

def gelu_value(pre):
    return 0.5 * pre * (1.0 + lax.erf(pre * root_half))

def gelu_slope(pre):
    return 0.5 * (1.0 + lax.erf(pre * root_half)) + pre * jnp.exp(-0.5 * pre * pre) * inv_root_tau

def widen(value):
    return lax.optimization_barrier(value.astype(jnp.bfloat16)).astype(jnp.float32)

def attend(item):
    query_rows, keys_in, value_rows = item
    scores = jnp.einsum('ihd,jhd->hij', query_rows.astype(jnp.float32), keys_in.astype(jnp.float32))
    top = lax.optimization_barrier(jnp.max(scores, axis=-1, keepdims=True))
    total = top + jnp.log(lax.optimization_barrier(jnp.sum(jnp.exp(scores - top), axis=-1, keepdims=True)))
    probs = jnp.exp(scores - total).astype(jnp.bfloat16)
    context_rows = jnp.einsum('hij,jhd->ihd', probs.astype(jnp.float32), value_rows.astype(jnp.float32))
    return (context_rows, total)

def attend_back(item):
    query_rows, keys_in, value_rows, total, context_grad = item
    scores = jnp.einsum('ihd,jhd->hij', query_rows.astype(jnp.float32), keys_in.astype(jnp.float32))
    probs = jnp.exp(scores - total)
    probs_half = probs.astype(jnp.bfloat16).astype(jnp.float32)
    upper_bound = context_grad.astype(jnp.float32)
    value_grad = jnp.einsum('hij,ihd->jhd', probs_half, upper_bound)
    prob_grad = jnp.einsum('ihd,jhd->hij', upper_bound, value_rows.astype(jnp.float32))
    inner = lax.optimization_barrier(jnp.sum(probs * prob_grad, axis=-1, keepdims=True))
    score_grad = (probs * (prob_grad - inner)).astype(jnp.bfloat16).astype(jnp.float32)
    query_grad = jnp.einsum('hij,jhd->ihd', score_grad, keys_in.astype(jnp.float32)) * 0.125
    key_grad = jnp.einsum('hij,ihd->jhd', score_grad, query_rows.astype(jnp.float32))
    return (query_grad, key_grad, value_grad)

def attention_forward(residual_stream, norm_gain, norm_shift, mix_half, project_half):
    half_width = jnp.bfloat16
    single = jnp.float32
    shape_heads = (TOKENS // SEQ, SEQ, HEADS, HEAD_DIM)
    centered_scaled, inverse_stddev = layer_normalize(residual_stream)
    normed_rows = (centered_scaled * norm_gain + norm_shift).astype(half_width)
    mixed = jnp.dot(normed_rows, mix_half, preferred_element_type=single)
    query_rows = (mixed[:, :D] * 0.125).astype(half_width).reshape(shape_heads)
    key_rows_full = mixed[:, D:2 * D].astype(half_width).reshape(shape_heads)
    value_rows = mixed[:, 2 * D:].astype(half_width).reshape(shape_heads)
    context_full, running_totals = lax.map(attend, (query_rows, key_rows_full, value_rows))
    context_rows = context_full.reshape(TOKENS, D).astype(half_width)
    after_residual = residual_stream + jnp.dot(context_rows, project_half, preferred_element_type=single)
    return (after_residual, (centered_scaled, inverse_stddev, normed_rows, query_rows, key_rows_full, value_rows, running_totals, context_rows))

def attention_backward(after_residual_grad, saved_activations, norm_gain, mix_half, project_half):
    half_width = jnp.bfloat16
    single = jnp.float32
    shape_heads = (TOKENS // SEQ, SEQ, HEADS, HEAD_DIM)
    centered_scaled, inverse_stddev, normed_rows, query_rows, key_rows_full, value_rows, running_totals, context_rows = saved_activations
    attn_half = after_residual_grad.astype(half_width)
    project_grad = jnp.dot(context_rows.T, attn_half, preferred_element_type=single)
    context_grad = jnp.dot(attn_half, project_half.T, preferred_element_type=single).astype(half_width).reshape(shape_heads)
    query_grad, key_grad, value_grad = lax.map(attend_back, (query_rows, key_rows_full, value_rows, running_totals, context_grad))
    mixed_grad = jnp.concatenate([query_grad.reshape(TOKENS, D), key_grad.reshape(TOKENS, D), value_grad.reshape(TOKENS, D)], axis=1).astype(half_width)
    mix_grad = jnp.dot(normed_rows.T, mixed_grad, preferred_element_type=single)
    normed_rows_grad = jnp.dot(mixed_grad, mix_half.T, preferred_element_type=single)
    norm_input_grad = jnp.stack([lax.optimization_barrier(jnp.sum(normed_rows_grad * centered_scaled, axis=0)), lax.optimization_barrier(jnp.sum(normed_rows_grad, axis=0))])
    token_input_grad = after_residual_grad + norm_backward_pass(normed_rows_grad, centered_scaled, inverse_stddev, norm_gain)
    return (token_input_grad, norm_input_grad, mix_grad, project_grad)

def slot_targets(block_routes):
    flat = block_routes.reshape(-1)
    onehot = (flat[:, None] == jnp.arange(EXPERTS, dtype=jnp.int32)[None, :]).astype(jnp.int32)
    position = jnp.cumsum(onehot, axis=0) - 1
    return (flat * CAP + lax.optimization_barrier(jnp.sum(onehot * position, axis=1))).astype(jnp.int32)

def fill_slots(targets, rows):
    return jnp.zeros((EXPERTS * CAP, D), jnp.bfloat16).at[targets].set(rows)

def to_experts(buffers):
    return buffers.reshape(DEVICES, EXPERTS, CAP, D).transpose(1, 0, 2, 3).reshape(EXPERTS, DEVICES * CAP, D)

def to_blocks(buffers):
    return buffers.reshape(EXPERTS, DEVICES, CAP, D).transpose(1, 0, 2, 3).reshape(DEVICES, EXPERTS * CAP, D)

def adam_step(param, state, grad, rate, decay):
    first = beta_one * state[0] + (1.0 - beta_one) * grad
    second = beta_two * state[1] + (1.0 - beta_two) * grad * grad
    update = first / (1.0 - beta_one ** STEP) / (jnp.sqrt(second / (1.0 - beta_two ** STEP)) + adam_eps)
    return (grad, param - rate * (update + decay * param), jnp.stack([first, second]))

def reference(tokens, routes, cotangent, lead_norm_one, lead_norm_one_state, lead_mix, lead_mix_state, lead_project, lead_project_state, lead_norm_two, lead_norm_two_state, lead_up, lead_up_state, lead_down, lead_down_state, norm_first, norm_first_state, mix_weight, mix_state, project_weight, project_state, norm_second, norm_second_state, router_weight, router_state, expert_in, expert_in_state, expert_out, expert_out_state):
    half_width = jnp.bfloat16
    single = jnp.float32
    lead_mix_half = lead_mix.astype(half_width)
    lead_project_half = lead_project.astype(half_width)
    lead_up_half = lead_up.astype(half_width)
    lead_down_half = lead_down.astype(half_width)
    mix_half = mix_weight.astype(half_width)
    project_half = project_weight.astype(half_width)
    router_half = router_weight.astype(half_width)
    in_half = expert_in.astype(half_width)
    out_half = expert_out.astype(half_width)
    lead_gain_one = widen(lead_norm_one[0])
    lead_shift_one = widen(lead_norm_one[1])
    leading_second_gain = widen(lead_norm_two[0])
    leading_second_shift = widen(lead_norm_two[1])
    gain_one = widen(norm_first[0])
    shift_one = widen(norm_first[1])
    second_norm_gain = widen(norm_second[0])
    second_norm_shift = widen(norm_second[1])
    after_first_residual, saved_a = attention_forward(tokens.astype(single), lead_gain_one, lead_shift_one, lead_mix_half, lead_project_half)
    second_centered_scaled, inverse_stddev_second = layer_normalize(after_first_residual)
    second_normed_rows = (second_centered_scaled * leading_second_gain + leading_second_shift).astype(half_width)
    up_pre = jnp.dot(second_normed_rows, lead_up_half, preferred_element_type=single)
    up_hidden = gelu_value(up_pre).astype(half_width)
    layer_one = after_first_residual + jnp.dot(up_hidden, lead_down_half, preferred_element_type=single)
    after_attention_sum, saved_one = attention_forward(layer_one, gain_one, shift_one, mix_half, project_half)
    lead_centered_scaled, inverse_stddev_lead = layer_normalize(after_attention_sum)
    lead_normed_rows = (lead_centered_scaled * second_norm_gain + second_norm_shift).astype(half_width)
    logits = jnp.dot(lead_normed_rows, router_half, preferred_element_type=single)
    chosen = jnp.take_along_axis(logits, routes, axis=1)
    gate_first = 1.0 / (1.0 + jnp.exp(chosen[:, 1] - chosen[:, 0]))
    gate_second = 1.0 / (1.0 + jnp.exp(chosen[:, 0] - chosen[:, 1]))
    gates = jnp.stack([gate_first, gate_second], axis=1)
    targets = jax.vmap(slot_targets)(routes.reshape(DEVICES, TOK_DEV, 2))
    slot_rows = jnp.repeat(lead_normed_rows.reshape(DEVICES, TOK_DEV, D), 2, axis=1)
    by_expert = to_experts(jax.vmap(fill_slots)(targets, slot_rows))

    def expert_forward(item):
        rows, first, second = item
        pre = jnp.dot(rows, first, preferred_element_type=single)
        hidden = gelu_value(pre).astype(half_width)
        return (jnp.dot(hidden, second, preferred_element_type=single).astype(half_width), pre)
    produced, pre_all = lax.map(expert_forward, (by_expert, in_half, out_half))
    outputs = jax.vmap(lambda buffer, target: buffer[target])(to_blocks(produced), targets)
    outputs = outputs.reshape(TOKENS, 2, D).astype(single)
    block = after_attention_sum + gates[:, 0:1] * outputs[:, 0] + gates[:, 1:2] * outputs[:, 1]
    block_out = block.astype(half_width)
    upstream_gradient = cotangent.astype(single)
    gate_grad = lax.optimization_barrier(jnp.sum(upstream_gradient[:, None, :] * outputs, axis=2))
    row_cot = (gates[:, :, None] * upstream_gradient[:, None, :]).astype(half_width)
    grad_by_expert = to_experts(jax.vmap(fill_slots)(targets, row_cot.reshape(DEVICES, 2 * TOK_DEV, D)))

    def expert_backward(item):
        rows, slot_grad, pre, first, second = item
        hidden = gelu_value(pre).astype(half_width)
        hidden_grad = jnp.dot(slot_grad, second.T, preferred_element_type=single)
        pre_grad = (hidden_grad * gelu_slope(pre)).astype(half_width)
        second_grad = jnp.dot(hidden.T, slot_grad, preferred_element_type=single)
        first_grad = jnp.dot(rows.T, pre_grad, preferred_element_type=single)
        row_grad = jnp.dot(pre_grad, first.T, preferred_element_type=single).astype(half_width)
        return (row_grad, first_grad, second_grad)
    row_grads, expert_in_grad, expert_out_grad = lax.map(expert_backward, (by_expert, grad_by_expert, pre_all, in_half, out_half))
    back_rows = jax.vmap(lambda buffer, target: buffer[target])(to_blocks(row_grads), targets)
    back_rows = back_rows.reshape(TOKENS, 2, D).astype(single)
    expert_ids = jnp.arange(EXPERTS, dtype=jnp.int32)
    logit_pair = gate_first * gate_second * (gate_grad[:, 0] - gate_grad[:, 1])
    columns = (routes[:, 0:1] == expert_ids[None, :]).astype(single) - (routes[:, 1:2] == expert_ids[None, :]).astype(single)
    logit_grad = (logit_pair[:, None] * columns).astype(half_width)
    router_grad = jnp.dot(lead_normed_rows.T, logit_grad, preferred_element_type=single)
    lead_normed_rows_grad = back_rows[:, 0] + back_rows[:, 1] + jnp.dot(logit_grad, router_half.T, preferred_element_type=single)
    second_norm_param_grad = jnp.stack([lax.optimization_barrier(jnp.sum(lead_normed_rows_grad * lead_centered_scaled, axis=0)), lax.optimization_barrier(jnp.sum(lead_normed_rows_grad, axis=0))])
    attention_output_grad = upstream_gradient + norm_backward_pass(lead_normed_rows_grad, lead_centered_scaled, inverse_stddev_lead, second_norm_gain)
    first_layer_grad, norm_first_grad, mix_grad, project_grad = attention_backward(attention_output_grad, saved_one, gain_one, mix_half, project_half)
    layer_one_half = first_layer_grad.astype(half_width)
    lead_down_grad = jnp.dot(up_hidden.T, layer_one_half, preferred_element_type=single)
    up_hidden_grad = jnp.dot(layer_one_half, lead_down_half.T, preferred_element_type=single)
    up_pre_grad = (up_hidden_grad * gelu_slope(up_pre)).astype(half_width)
    lead_up_grad = jnp.dot(second_normed_rows.T, up_pre_grad, preferred_element_type=single)
    second_normed_rows_grad = jnp.dot(up_pre_grad, lead_up_half.T, preferred_element_type=single)
    leading_second_norm_grad = jnp.stack([lax.optimization_barrier(jnp.sum(second_normed_rows_grad * second_centered_scaled, axis=0)), lax.optimization_barrier(jnp.sum(second_normed_rows_grad, axis=0))])
    after_first_residual_grad = first_layer_grad + norm_backward_pass(second_normed_rows_grad, second_centered_scaled, inverse_stddev_second, leading_second_gain)
    token_input_grad, lead_norm_one_grad, lead_mix_grad, lead_project_grad = attention_backward(after_first_residual_grad, saved_a, lead_gain_one, lead_mix_half, lead_project_half)
    return (block_out, token_input_grad) + adam_step(lead_norm_one, lead_norm_one_state, lead_norm_one_grad, norm_rate, 0.0) + adam_step(lead_mix, lead_mix_state, lead_mix_grad, matrix_rate, decay_rate) + adam_step(lead_project, lead_project_state, lead_project_grad, matrix_rate, decay_rate) + adam_step(lead_norm_two, lead_norm_two_state, leading_second_norm_grad, norm_rate, 0.0) + adam_step(lead_up, lead_up_state, lead_up_grad, matrix_rate, decay_rate) + adam_step(lead_down, lead_down_state, lead_down_grad, matrix_rate, decay_rate) + adam_step(norm_first, norm_first_state, norm_first_grad, norm_rate, 0.0) + adam_step(mix_weight, mix_state, mix_grad, matrix_rate, decay_rate) + adam_step(project_weight, project_state, project_grad, matrix_rate, decay_rate) + adam_step(norm_second, norm_second_state, second_norm_param_grad, norm_rate, 0.0) + adam_step(router_weight, router_state, router_grad, matrix_rate, decay_rate) + adam_step(expert_in, expert_in_state, expert_in_grad, matrix_rate, decay_rate) + adam_step(expert_out, expert_out_state, expert_out_grad, matrix_rate, decay_rate)
```

```python
import functools

import jax
import jax.numpy as jnp
from jax import lax
from jax.experimental import pallas as pl
from jax.experimental.pallas import tpu as pltpu
from jax.sharding import PartitionSpec as P

HEADS = 12
HEAD_DIM = 64
SEQ = 197
STEP = 3


norm_eps = 1e-06
beta_one = 0.9
beta_two = 0.999
adam_eps = 1e-08
matrix_rate = 0.03
norm_rate = 0.3
decay_rate = 0.05
root_half = 0.7071067811865476
inv_root_tau = 0.3989422804014327


def layer_normalize(rows):
    center = jnp.mean(rows, axis=-1, keepdims=True)
    offset = rows - center
    spread = jnp.mean(offset * offset, axis=-1, keepdims=True)
    inverse_stddev = lax.rsqrt(spread + norm_eps)
    return (offset * inverse_stddev, inverse_stddev)


def norm_backward_pass(upper_bound, centered_scaled, inverse_stddev, norm_gain):
    scaled_rows = upper_bound * norm_gain
    return inverse_stddev * (
        scaled_rows
        - jnp.mean(scaled_rows, axis=-1, keepdims=True)
        - centered_scaled * jnp.mean(scaled_rows * centered_scaled, axis=-1, keepdims=True)
    )


def gelu_value(pre):
    return 0.5 * pre * (1.0 + lax.erf(pre * root_half))


def gelu_slope(pre):
    return 0.5 * (1.0 + lax.erf(pre * root_half)) + pre * jnp.exp(-0.5 * pre * pre) * inv_root_tau


def attend(query_rows, keys_in, value_rows):
    scores = jnp.einsum("ihd,jhd->hij", query_rows, keys_in, preferred_element_type=jnp.float32)
    top = jnp.max(scores, axis=-1, keepdims=True)
    total = top + jnp.log(jnp.sum(jnp.exp(scores - top), axis=-1, keepdims=True))
    probs = jnp.exp(scores - total).astype(jnp.bfloat16)
    context_rows = jnp.einsum("hij,jhd->ihd", probs, value_rows, preferred_element_type=jnp.float32)
    return (context_rows, total)


def attend_back(query_rows, keys_in, value_rows, total, context_grad):
    scores = jnp.einsum("ihd,jhd->hij", query_rows, keys_in, preferred_element_type=jnp.float32)
    probs = jnp.exp(scores - total)
    probs_half = probs.astype(jnp.bfloat16)
    value_grad = jnp.einsum(
        "hij,ihd->jhd", probs_half, context_grad, preferred_element_type=jnp.float32
    )
    prob_grad = jnp.einsum(
        "ihd,jhd->hij", context_grad, value_rows, preferred_element_type=jnp.float32
    )
    inner = jnp.sum(probs * prob_grad, axis=-1, keepdims=True)
    score_grad = (probs * (prob_grad - inner)).astype(jnp.bfloat16)
    query_grad = (
        jnp.einsum("hij,jhd->ihd", score_grad, keys_in, preferred_element_type=jnp.float32) * 0.125
    )
    key_grad = jnp.einsum(
        "hij,ihd->jhd", score_grad, query_rows, preferred_element_type=jnp.float32
    )
    return (query_grad, key_grad, value_grad)


def attention_forward(residual_stream, norm_gain, norm_shift, mix_half, project_half):
    half_width = jnp.bfloat16
    single = jnp.float32
    count = residual_stream.shape[0]
    width = residual_stream.shape[1]
    shape_heads = (count // SEQ, SEQ, HEADS, HEAD_DIM)
    centered_scaled, inverse_stddev = layer_normalize(residual_stream)
    normed_rows = (centered_scaled * norm_gain + norm_shift).astype(half_width)
    mixed = jnp.dot(normed_rows, mix_half, preferred_element_type=single)
    query_rows = (mixed[:, :width] * 0.125).astype(half_width).reshape(shape_heads)
    key_rows_full = mixed[:, width : 2 * width].astype(half_width).reshape(shape_heads)
    value_rows = mixed[:, 2 * width :].astype(half_width).reshape(shape_heads)
    context_full, running_totals = jax.vmap(attend)(query_rows, key_rows_full, value_rows)
    context_rows = context_full.reshape(count, width).astype(half_width)
    after_residual = residual_stream + jnp.dot(
        context_rows, project_half, preferred_element_type=single
    )
    return (
        after_residual,
        (
            centered_scaled,
            inverse_stddev,
            normed_rows,
            query_rows,
            key_rows_full,
            value_rows,
            running_totals,
            context_rows,
        ),
    )


def attention_backward(after_residual_grad, saved_activations, norm_gain, mix_half, project_half):
    half_width = jnp.bfloat16
    single = jnp.float32
    (
        centered_scaled,
        inverse_stddev,
        normed_rows,
        query_rows,
        key_rows_full,
        value_rows,
        running_totals,
        context_rows,
    ) = saved_activations
    count = after_residual_grad.shape[0]
    width = after_residual_grad.shape[1]
    attn_half = after_residual_grad.astype(half_width)
    project_grad = jnp.einsum("td,te->de", context_rows, attn_half, preferred_element_type=single)
    context_grad = (
        jnp.einsum("te,de->td", attn_half, project_half, preferred_element_type=single)
        .astype(half_width)
        .reshape(query_rows.shape)
    )
    query_grad, key_grad, value_grad = jax.vmap(attend_back)(
        query_rows, key_rows_full, value_rows, running_totals, context_grad
    )
    mixed_grad = jnp.concatenate(
        [
            query_grad.reshape(count, width),
            key_grad.reshape(count, width),
            value_grad.reshape(count, width),
        ],
        axis=1,
    ).astype(half_width)
    mix_grad = jnp.einsum("td,te->de", normed_rows, mixed_grad, preferred_element_type=single)
    normed_rows_grad = jnp.einsum("te,de->td", mixed_grad, mix_half, preferred_element_type=single)
    norm_input_grad = jnp.stack(
        [jnp.sum(normed_rows_grad * centered_scaled, axis=0), jnp.sum(normed_rows_grad, axis=0)]
    )
    token_input_grad = after_residual_grad + norm_backward_pass(
        normed_rows_grad, centered_scaled, inverse_stddev, norm_gain
    )
    return (token_input_grad, norm_input_grad, mix_grad, project_grad)


def dot_nn(a, b):
    return lax.dot_general(a, b, (((1,), (0,)), ((), ())), preferred_element_type=jnp.float32)


def dot_nt(a, b):
    return lax.dot_general(a, b, (((1,), (1,)), ((), ())), preferred_element_type=jnp.float32)


def dot_tn(a, b):
    return lax.dot_general(a, b, (((0,), (0,)), ((), ())), preferred_element_type=jnp.float32)


MESH = pl.DeviceIdType.MESH
BLK = 384
ROWS = 96
BIG = 3 * BLK - 256


def place():
    dp, e = lax.axis_index("dp"), lax.axis_index("expert")
    return dp, e, dp // 2, lax.rem(dp, 2), e // 4, lax.rem(e, 4)


def send(src, dst, send_sem, recv_sem, device):
    return pltpu.make_async_remote_copy(
        src_ref=src,
        dst_ref=dst,
        send_sem=send_sem,
        recv_sem=recv_sem,
        device_id=device,
        device_id_type=MESH,
    )


def meet():
    dp, e, z, c, _, _ = place()
    barrier = pltpu.get_barrier_semaphore()

    def greet(k, carry):
        pl.semaphore_signal(
            barrier, inc=1, device_id=(dp, lax.rem(e + k, 16)), device_id_type=MESH
        )
        return carry

    lax.fori_loop(1, 16, greet, 0)
    for k in range(1, 4):
        pl.semaphore_signal(
            barrier, inc=1, device_id=(2 * lax.rem(z + k, 4) + c, e), device_id_type=MESH
        )
    pl.semaphore_signal(barrier, inc=1, device_id=(2 * z + 1 - c, e), device_id_type=MESH)
    pl.semaphore_wait(barrier, 19)


def cell(path, first, second):
    _, _, _, _, y, x = place()
    dy, dx = (second, first) if path == 0 else (first, second)
    return lax.rem(y + dy, 4) * 4 + lax.rem(x + dx, 4)


def columns(block):
    return pl.ds(pl.multiple_of(block * BLK, BLK), BLK)


def swap_plane(source, target, send_sem, recv_sem):
    dp, e, _, _, _, _ = place()

    def one(k):
        peer = lax.rem(e + k, 16)
        return send(source.at[peer], target.at[e], send_sem.at[k], recv_sem.at[k], (dp, peer))

    def begin(k, carry):
        one(k).start()
        return carry

    def finish(k, carry):
        one(k).wait()
        return carry

    lax.fori_loop(1, 16, begin, 0)
    target[e] = source[e]
    lax.fori_loop(1, 16, finish, 0)


def six_of_eight(shape, row_dim):
    row = lax.broadcasted_iota(jnp.int32, shape, row_dim)
    col = lax.broadcasted_iota(jnp.int32, shape, 1 - row_dim)
    inner = jnp.bitwise_and(col, 7)
    same = (row == 6 * lax.shift_right_logical(col, 3) + inner) & (inner < 6)
    return jnp.where(same, 1.0, 0.0).astype(jnp.bfloat16)


def pieces(refs):
    lead_mix, lead_project, mix, project = refs
    for p in range(16):
        ref, at = ((lead_mix, 0), (lead_project, 6), (mix, 8), (project, 14))[
            0 if p < 6 else 1 if p < 8 else 2 if p < 14 else 3
        ]
        yield p, ref, slice((p - at) * BLK, (p - at + 1) * BLK)


def gather_kernel(
    lead_mix, lead_project, mix, project, small, dense,
    ga, gf, gs,
    wide, came, tower, s1, r1, s2, r2, s3, r3, s4, r4, local,
):
    dp, e, z, c, y, x = place()
    sibling = (2 * z + 1 - c, e)
    wide[...] = jnp.zeros_like(wide)
    for p, ref, cols in pieces((lead_mix, lead_project, mix, project)):
        wide[p, 0:6, 0:BLK] = ref[:, cols]
        wide[p, 0:6, BLK:512] = small[...]
    meet()
    swap_plane(wide, came, s1, r1)
    rows = came[...].reshape(128, 512).astype(jnp.bfloat16)
    pick = six_of_eight((ROWS, 128), 0)
    tower[z, :, 0:512] = jnp.dot(pick, rows, preferred_element_type=jnp.float32).astype(
        jnp.bfloat16
    )
    tower[z, :, 512:BIG] = dense[...]

    def climb(k):
        return send(
            tower.at[z], tower.at[z], s2.at[k], r2.at[k], (2 * lax.rem(z + k, 4) + c, e)
        )

    for k in (1, 3, 2):
        climb(k).start()
    for k in (1, 3, 2):
        climb(k).wait()

    full, low, high = pl.ds(0, 4), pl.ds(0, 2), pl.ds(2, 2)
    whole = (ga, gf)
    start = (0, 512)

    def neighbour(path, axis, step):
        along_x = (axis == 0) == (path == 0)
        dx, dy = (step, 0) if along_x else (0, step)
        return (dp, lax.rem(y + dy, 4) * 4 + lax.rem(x + dx, 4))

    def at(path, first, second, part=full):
        return whole[path].at[part, c, :, columns(cell(path, first, second))]

    def own(path):
        return tower.at[:, :, pl.ds(start[path], BLK)]

    def move(path, number, device, first, second, part=full, source=None):
        ref = at(path, first, second, part)
        return send(
            ref if source is None else source, ref, s3.at[path, number], r3.at[path, number], device
        )

    slots = (0, 3, 1, 2)
    begun = []

    def go(*args, **named):
        copy = move(*args, **named)
        copy.start()
        begun.append(copy)

    def arrived(path, number, first, second, part=full):
        move(path, number, sibling, first, second, part).wait_recv()

    def spread(path, j, source=None):
        first = slots[j]
        go(path, 4 + 4 * j, neighbour(path, 1, 1), first, 0, source=source)
        go(path, 5 + 4 * j, neighbour(path, 1, 3), first, 0, source=source)
        go(path, 20 + 4 * j, sibling, first, 0, source=source)

    keep = []
    for path in (0, 1):
        go(path, 0, neighbour(path, 0, 1), 0, 0, source=own(path))
        go(path, 1, neighbour(path, 0, 3), 0, 0, source=own(path))
    for path in (0, 1):
        spread(path, 0, source=own(path))
        copy = pltpu.make_async_copy(own(path), at(path, 0, 0), local.at[path])
        copy.start()
        keep.append(copy)
    minor = send(
        tower.at[:, :, pl.ds(BLK, 128)], gs.at[:, c], s4.at[0], r4.at[0], sibling
    )
    minor.start()
    copy = pltpu.make_async_copy(tower.at[:, :, pl.ds(BLK, 128)], gs.at[:, c], local.at[2])
    copy.start()
    keep.append(copy)
    for path in (0, 1):
        arrived(path, 0, 3, 0)
        go(path, 2, neighbour(path, 0, 1), 3, 0, low)
        arrived(path, 1, 1, 0)
        go(path, 3, neighbour(path, 0, 3), 1, 0, high)
    for path in (0, 1):
        spread(path, 1)
        spread(path, 2)
    for j in range(4):
        first = slots[j]
        if j == 1:
            for path in (0, 1):
                arrived(path, 2, 2, 0, low)
                arrived(path, 3, 2, 0, high)
                spread(path, 3)
        for path in (0, 1):
            arrived(path, 4 + 4 * j, first, 3)
            go(path, 6 + 4 * j, neighbour(path, 1, 1), first, 3, low)
            go(path, 21 + 4 * j, sibling, first, 3)
            arrived(path, 5 + 4 * j, first, 1)
            go(path, 7 + 4 * j, neighbour(path, 1, 3), first, 1, high)
            go(path, 22 + 4 * j, sibling, first, 1)
    for j in range(4):
        first = slots[j]
        for path in (0, 1):
            arrived(path, 6 + 4 * j, first, 2, low)
            arrived(path, 7 + 4 * j, first, 2, high)
            go(path, 23 + 4 * j, sibling, first, 2)
    for copy in keep:
        copy.wait()
    minor.wait()
    for copy in begun:
        copy.wait_send()
    for path in (0, 1):
        for number in range(20, 36):
            arrived(path, number, 0, 0)


def gather_weights(lead_mix, lead_project, mix, project, small, dense):
    half = jnp.bfloat16
    vmem = pl.BlockSpec(memory_space=pltpu.VMEM)
    hbm = pl.BlockSpec(memory_space=pl.ANY)
    dma = pltpu.SemaphoreType.DMA
    return pl.pallas_call(
        gather_kernel,
        out_shape=[
            jax.ShapeDtypeStruct((4, 2, ROWS, 16 * BLK), half),
            jax.ShapeDtypeStruct((4, 2, ROWS, 16 * BLK), half),
            jax.ShapeDtypeStruct((4, 2, ROWS, 128), half),
        ],
        in_specs=[vmem] * 6,
        out_specs=[hbm] * 3,
        scratch_shapes=[
            pltpu.VMEM((16, 8, 512), jnp.float32),
            pltpu.VMEM((16, 8, 512), jnp.float32),
            pltpu.VMEM((4, ROWS, BIG), half),
            dma((16,)), dma((16,)), dma((4,)), dma((4,)),
            dma((2, 36)), dma((2, 36)), dma((1,)), dma((1,)), dma((3,)),
        ],
        compiler_params=pltpu.CompilerParams(
            collective_id=0, has_side_effects=True, vmem_limit_bytes=16 * 2**20
        ),
    )(lead_mix, lead_project, mix, project, small, dense)


def scatter_kernel(
    da, df, ds,
    lead_mix, lead_project, mix, project, small, dense,
    acc, other, m1, m2, n1, n2, tower, layers, minor, wide, came,
    loc, ss, rs, t1, u1, t2, u2, v1, w1, v2, w2, s2, r2, s4, r4, s1, r1,
):
    single, half = jnp.float32, jnp.bfloat16
    dp, e, z, c, y, x = place()
    sibling = (2 * z + 1 - c, e)
    full, low, high = pl.ds(0, 4), pl.ds(0, 2), pl.ds(2, 2)
    parts = (da, df)
    order = (2, 1, 3, 0)

    def neighbour(path, axis, step):
        along_x = (axis == 0) == (path == 0)
        dx, dy = (step, 0) if along_x else (0, step)
        return (dp, lax.rem(y + dy, 4) * 4 + lax.rem(x + dx, 4))

    def block(path, first, second, part=full):
        return acc.at[path, part, :, columns(cell(path, first, second))]

    def load(path, first, second):
        cols = columns(cell(path, first, second))
        return pltpu.make_async_copy(
            parts[path].at[:, c, :, cols], acc.at[path, :, :, cols], loc.at[path, second, first]
        )

    def cross(path, first, second):
        cols = columns(cell(path, first, second))
        return send(
            parts[path].at[:, 1 - c, :, cols],
            other.at[path, :, :, cols],
            ss.at[path, second, first],
            rs.at[path, second, first],
            sibling,
        )

    loads = [(path, first, second) for second in order for path in (0, 1) for first in order]
    for spot in loads:
        load(*spot).start()
    meet()
    for spot in loads:
        cross(*spot).start()
    little = send(ds.at[:, 1 - c], minor.at[1], s4.at[0], r4.at[0], sibling)
    little.start()
    mine = pltpu.make_async_copy(ds.at[:, c], minor.at[0], s4.at[1])
    mine.start()

    def total(ref, *terms):
        value = ref[...].astype(single)
        for term in terms:
            value = value + term[...].astype(single)
        ref[...] = value.astype(half)

    def ready(path, first, second):
        load(path, first, second).wait()
        cross(path, first, second).wait()
        return other.at[path, :, :, columns(cell(path, first, second))]

    def far(path, first, up):
        return send(
            block(path, first, 2, low if up else high),
            m1.at[path, first, 0 if up else 1],
            t1.at[path, first, 0 if up else 1],
            u1.at[path, first, 0 if up else 1],
            neighbour(path, 1, 1 if up else 3),
        )

    def near(path, first, up):
        return send(
            block(path, first, 1 if up else 3),
            m2.at[path, first, 0 if up else 1],
            t2.at[path, first, 0 if up else 1],
            u2.at[path, first, 0 if up else 1],
            neighbour(path, 1, 1 if up else 3),
        )

    def last_far(path, up):
        return send(
            block(path, 2, 0, low if up else high),
            n1.at[path, 0 if up else 1],
            v1.at[path, 0 if up else 1],
            w1.at[path, 0 if up else 1],
            neighbour(path, 0, 1 if up else 3),
        )

    def last_near(path, up):
        return send(
            block(path, 1 if up else 3, 0),
            n2.at[path, 0 if up else 1],
            v2.at[path, 0 if up else 1],
            w2.at[path, 0 if up else 1],
            neighbour(path, 0, 1 if up else 3),
        )

    for path in (0, 1):
        for first in order:
            total(block(path, first, 2), ready(path, first, 2))
            far(path, first, True).start()
            far(path, first, False).start()
    for up in (True, False):
        second = 1 if up else 3
        for path in (0, 1):
            for first in order:
                term = ready(path, first, second)
                far(path, first, up).wait_recv()
                total(block(path, first, second), term)
                part = low if up else high
                total(block(path, first, second, part), m1.at[path, first, 0 if up else 1])
                near(path, first, up).start()
    for first in order:
        for path in (0, 1):
            term = ready(path, first, 0)
            near(path, first, True).wait_recv()
            near(path, first, False).wait_recv()
            total(block(path, first, 0), term, m2.at[path, first, 0], m2.at[path, first, 1])
            if first == 2:
                last_far(path, True).start()
                last_far(path, False).start()
            elif first != 0:
                up = first == 1
                last_far(path, up).wait_recv()
                part = low if up else high
                total(block(path, first, 0, part), n1.at[path, 0 if up else 1])
                last_near(path, up).start()
            else:
                last_near(path, True).wait_recv()
                last_near(path, False).wait_recv()
                total(block(path, 0, 0), n2.at[path, 0], n2.at[path, 1])
                lo = 0 if path == 0 else 512
                tower[:, :, lo : lo + BLK] = acc[path, :, :, columns(cell(path, 0, 0))]
    little.wait()
    mine.wait()
    tower[:, :, BLK:512] = (
        minor[0].astype(single) + minor[1].astype(single)
    ).astype(half)

    def fall(k):
        to = lax.rem(z + k, 4)
        return send(tower.at[to], layers.at[k], s2.at[k], r2.at[k], (2 * to + c, e))

    for k in (1, 3, 2):
        fall(k).start()
    value = tower[z].astype(single)
    for k in (1, 3, 2):
        fall(k).wait()
        value = value + layers[k].astype(single)
    dense[...] = value[:, 512:BIG]
    rows = value[:, 0:512]
    upper = rows.astype(half)
    lower = (rows - upper.astype(single)).astype(half)
    pick = six_of_eight((128, ROWS), 1)
    wide[...] = (
        jnp.dot(pick, upper, preferred_element_type=single)
        + jnp.dot(pick, lower, preferred_element_type=single)
    ).reshape(16, 8, 512)
    swap_plane(wide, came, s1, r1)
    for p, ref, cols in pieces((lead_mix, lead_project, mix, project)):
        ref[:, cols] = came[p, 0:6, 0:BLK]
    small[...] = jnp.sum(came[:, 0:6, BLK:512], axis=0)
    for path in (0, 1):
        for first in order:
            for up in (True, False):
                far(path, first, up).wait_send()
                near(path, first, up).wait_send()
        for up in (True, False):
            last_far(path, up).wait_send()
            last_near(path, up).wait_send()


def scatter_grads(da, df, ds):
    half, single = jnp.bfloat16, jnp.float32
    vmem = pl.BlockSpec(memory_space=pltpu.VMEM)
    hbm = pl.BlockSpec(memory_space=pl.ANY)
    dma = pltpu.SemaphoreType.DMA
    shape = jax.ShapeDtypeStruct
    return pl.pallas_call(
        scatter_kernel,
        out_shape=[
            shape((6, 2304), single), shape((6, 768), single),
            shape((6, 2304), single), shape((6, 768), single),
            shape((6, 128), single), shape((ROWS, BLK), single),
        ],
        in_specs=[hbm] * 3,
        out_specs=[vmem] * 6,
        scratch_shapes=[
            pltpu.VMEM((2, 4, ROWS, 16 * BLK), half),
            pltpu.VMEM((2, 4, ROWS, 16 * BLK), half),
            pltpu.VMEM((2, 4, 2, 2, ROWS, BLK), half),
            pltpu.VMEM((2, 4, 2, 4, ROWS, BLK), half),
            pltpu.VMEM((2, 2, 2, ROWS, BLK), half),
            pltpu.VMEM((2, 2, 4, ROWS, BLK), half),
            pltpu.VMEM((4, ROWS, BIG), half),
            pltpu.VMEM((4, ROWS, BIG), half),
            pltpu.VMEM((2, 4, ROWS, 128), half),
            pltpu.VMEM((16, 8, 512), single),
            pltpu.VMEM((16, 8, 512), single),
            dma((2, 4, 4)), dma((2, 4, 4)), dma((2, 4, 4)),
            dma((2, 4, 2)), dma((2, 4, 2)), dma((2, 4, 2)), dma((2, 4, 2)),
            dma((2, 2)), dma((2, 2)), dma((2, 2)), dma((2, 2)),
            dma((4,)), dma((4,)), dma((2,)), dma((2,)), dma((16,)), dma((16,)),
        ],
        compiler_params=pltpu.CompilerParams(
            collective_id=1, has_side_effects=True, vmem_limit_bytes=48 * 2**20
        ),
    )(da, df, ds)


PADDED = 208


def nn(a, b):
    return jnp.dot(a, b, preferred_element_type=jnp.float32)


def nt(a, b):
    return lax.dot_general(a, b, (((1,), (1,)), ((), ())), preferred_element_type=jnp.float32)


def tn(a, b):
    return lax.dot_general(a, b, (((0,), (0,)), ((), ())), preferred_element_type=jnp.float32)


def half_turn(value):
    return pltpu.roll(value, BLK // 2, 1)


def left_half(value):
    lane = lax.broadcasted_iota(jnp.int32, value.shape, 1)
    return jnp.where(lane < BLK // 2, value, 0.0)


def dense_forward_kernel(rows, norm, both, out, pre_out, normed):
    half = jnp.bfloat16

    @pl.when(pl.program_id(0) == 0)
    def _():
        xhat, _ = layer_normalize(rows[...])
        normed[...] = (xhat * norm[0:1, :] + norm[1:2, :]).astype(half)
        out[...] = rows[...]

    pre = nn(normed[...], both[...])
    pre_out[...] = pre
    hidden = half_turn(left_half(gelu_value(pre))).astype(half)
    out[...] += nt(hidden, both[...])


def dense_backward_kernel(grad, rows, norm, pre, both, out, both_grad, norm_grad, normed, low, acc):
    half = jnp.bfloat16
    step = pl.program_id(0)

    @pl.when(step == 0)
    def _():
        xhat, _ = layer_normalize(rows[...])
        normed[...] = (xhat * norm[0:1, :] + norm[1:2, :]).astype(half)
        low[...] = grad[...].astype(half)
        acc[...] = jnp.zeros_like(acc)

    value = pre[...]
    hidden = half_turn(left_half(gelu_value(value))).astype(half)
    hidden_grad = half_turn(nn(low[...], both[...]))
    pre_grad = left_half(hidden_grad * gelu_slope(value)).astype(half)
    both_grad[...] = (tn(normed[...], pre_grad) + tn(low[...], hidden)).astype(half)
    acc[...] += nt(pre_grad, both[...])

    @pl.when(step == pl.num_programs(0) - 1)
    def _():
        xhat, inverse = layer_normalize(rows[...])
        total = acc[...]
        norm_grad[0:1, :] = jnp.sum(total * xhat, axis=0, keepdims=True)
        norm_grad[1:2, :] = jnp.sum(total, axis=0, keepdims=True)
        out[...] = grad[...] + norm_backward_pass(total, xhat, inverse, norm[0:1, :])


def dense_forward(rows, norm, both):
    single = jnp.float32
    depth, wide = both.shape
    shape = jax.ShapeDtypeStruct
    still = lambda i: (0, 0)
    return pl.pallas_call(
        dense_forward_kernel,
        grid=(wide // BLK,),
        out_shape=[shape((PADDED, depth), single), shape((PADDED, wide), single)],
        in_specs=[
            pl.BlockSpec((PADDED, depth), still),
            pl.BlockSpec((2, depth), still),
            pl.BlockSpec((depth, BLK), lambda i: (0, i)),
        ],
        out_specs=[
            pl.BlockSpec((PADDED, depth), still),
            pl.BlockSpec((PADDED, BLK), lambda i: (0, i)),
        ],
        scratch_shapes=[pltpu.VMEM((PADDED, depth), jnp.bfloat16)],
        compiler_params=pltpu.CompilerParams(vmem_limit_bytes=32 * 2**20),
    )(rows, norm, both)


def dense_backward(grad, rows, norm, pre, both):
    single, half = jnp.float32, jnp.bfloat16
    depth, wide = both.shape
    shape = jax.ShapeDtypeStruct
    still = lambda i: (0, 0)
    return pl.pallas_call(
        dense_backward_kernel,
        grid=(wide // BLK,),
        out_shape=[
            shape((PADDED, depth), single),
            shape((depth, wide), half),
            shape((2, depth), single),
        ],
        in_specs=[
            pl.BlockSpec((PADDED, depth), still),
            pl.BlockSpec((PADDED, depth), still),
            pl.BlockSpec((2, depth), still),
            pl.BlockSpec((PADDED, BLK), lambda i: (0, i)),
            pl.BlockSpec((depth, BLK), lambda i: (0, i)),
        ],
        out_specs=[
            pl.BlockSpec((PADDED, depth), still),
            pl.BlockSpec((depth, BLK), lambda i: (0, i)),
            pl.BlockSpec((2, depth), still),
        ],
        scratch_shapes=[
            pltpu.VMEM((PADDED, depth), half),
            pltpu.VMEM((PADDED, depth), half),
            pltpu.VMEM((PADDED, depth), single),
        ],
        compiler_params=pltpu.CompilerParams(vmem_limit_bytes=32 * 2**20),
    )(grad, rows, norm, pre, both)


def expert_kernel(rows, cot, w_in, w_out, made, back, in_grad, out_grad, acc, back_acc):
    half = jnp.bfloat16
    step = pl.program_id(0)

    @pl.when(step == 0)
    def _():
        acc[...] = jnp.zeros_like(acc)
        back_acc[...] = jnp.zeros_like(back_acc)

    pre = nn(rows[...], w_in[0])
    hidden = gelu_value(pre).astype(half)
    acc[...] += nn(hidden, w_out[0])
    pre_grad = (nt(cot[...], w_out[0]) * gelu_slope(pre)).astype(half)
    back_acc[...] += nt(pre_grad, w_in[0])
    in_grad[0] = tn(rows[...], pre_grad).astype(half)
    out_grad[0] = tn(hidden, cot[...]).astype(half)

    @pl.when(step == pl.num_programs(0) - 1)
    def _():
        made[...] = acc[...].astype(half)
        back[...] = back_acc[...].astype(half)


def expert_pass(rows, cot, w_in, w_out):
    half, single = jnp.bfloat16, jnp.float32
    count, depth = rows.shape
    parts, _, inner = w_in.shape
    shape = jax.ShapeDtypeStruct
    whole = pl.BlockSpec((count, depth), lambda i: (0, 0))
    inward = pl.BlockSpec((1, depth, inner), lambda i: (i, 0, 0))
    outward = pl.BlockSpec((1, inner, depth), lambda i: (i, 0, 0))
    return pl.pallas_call(
        expert_kernel,
        grid=(parts,),
        out_shape=[
            shape((count, depth), half), shape((count, depth), half),
            shape(w_in.shape, half), shape(w_out.shape, half),
        ],
        in_specs=[whole, whole, inward, outward],
        out_specs=[whole, whole, inward, outward],
        scratch_shapes=[pltpu.VMEM((count, depth), single)] * 2,
        compiler_params=pltpu.CompilerParams(vmem_limit_bytes=40 * 2**20),
    )(rows, cot, w_in, w_out)


def adam_kernel(rates, *refs):
    count = len(rates)
    params, states, grads = refs[:count], refs[count : 2 * count], refs[2 * count : 3 * count]
    outs = refs[3 * count :]
    for k, (rate, decay) in enumerate(rates):
        grad = grads[k][...].astype(jnp.float32)
        param, first, second = params[k][...], states[k][0], states[k][1]
        first = beta_one * first + (1.0 - beta_one) * grad
        second = beta_two * second + (1.0 - beta_two) * grad * grad
        update = (
            first
            / (1.0 - beta_one**STEP)
            / (jnp.sqrt(second / (1.0 - beta_two**STEP)) + adam_eps)
        )
        outs[3 * k][...] = grad
        outs[3 * k + 1][...] = param - rate * (update + decay * param)
        outs[3 * k + 2][0] = first
        outs[3 * k + 2][1] = second


def adam_all(params, states, grads, rates):
    single = jnp.float32
    vmem = pl.BlockSpec(memory_space=pltpu.VMEM)
    shape = jax.ShapeDtypeStruct
    outs = []
    for param, state in zip(params, states):
        outs += [shape(param.shape, single), shape(param.shape, single), shape(state.shape, single)]
    return pl.pallas_call(
        functools.partial(adam_kernel, rates),
        out_shape=outs,
        in_specs=[vmem] * (3 * len(params)),
        out_specs=[vmem] * len(outs),
        compiler_params=pltpu.CompilerParams(vmem_limit_bytes=40 * 2**20),
    )(*params, *states, *grads)


def body(
    tokens,
    routes,
    cotangent,
    lead_norm_one,
    lead_norm_one_state,
    lead_mix,
    lead_mix_state,
    lead_project,
    lead_project_state,
    lead_norm_two,
    lead_norm_two_state,
    lead_up,
    lead_up_state,
    lead_down,
    lead_down_state,
    norm_first,
    norm_first_state,
    mix_weight,
    mix_state,
    project_weight,
    project_state,
    norm_second,
    norm_second_state,
    router_weight,
    router_state,
    expert_in,
    expert_in_state,
    expert_out,
    expert_out_state,
):
    half = jnp.bfloat16
    single = jnp.float32
    count, width = tokens.shape
    experts = router_weight.shape[1]
    planes = lax.axis_size("expert")
    slot_rows = 32
    small = jnp.concatenate(
        [lead_norm_one.T, lead_norm_two.T, norm_first.T, norm_second.T, router_weight], axis=1
    )
    small = jnp.pad(small, ((0, 0), (0, 128 - small.shape[1])))
    dense = jnp.concatenate([lead_up, lead_down.T], axis=1).astype(half)
    own_full, dense_full, small_full = gather_weights(
        lead_mix, lead_project, mix_weight, project_weight, small, dense
    )
    own_full = own_full.reshape(width, -1)
    dense_full = dense_full.reshape(width, -1)
    small_full = small_full.reshape(width, -1)
    in_full = lax.all_gather(expert_in[0].astype(half), "dp", axis=0)
    out_full = lax.all_gather(expert_out[0].astype(half), "dp", axis=0)
    lead_mix_half = own_full[:, : 3 * width]
    lead_project_half = own_full[:, 3 * width : 4 * width]
    mix_half = own_full[:, 4 * width : 7 * width]
    project_half = own_full[:, 7 * width :]
    norms = small_full[:, :8].T.astype(single)
    router_half = small_full[:, 8:24]
    after_a, saved_a = attention_forward(
        tokens.astype(single), norms[0], norms[1], lead_mix_half, lead_project_half
    )
    extra = ((0, PADDED - count), (0, 0))
    after_a = jnp.pad(after_a, extra)
    layer_one, up_pre = dense_forward(after_a, norms[2:4], dense_full)
    layer_one = layer_one[:count]
    after_attn, saved_one = attention_forward(
        layer_one, norms[4], norms[5], mix_half, project_half
    )
    xhat_two, inv_two = layer_normalize(after_attn)
    normed_two = (xhat_two * norms[6] + norms[7]).astype(half)
    logits = dot_nn(normed_two, router_half)
    ids = jnp.arange(experts, dtype=jnp.int32)
    picks = [(routes[:, k : k + 1] == ids[None, :]).astype(single) for k in range(2)]
    level = [jnp.sum(p * logits, axis=1, keepdims=True) for p in picks]
    gates = [
        1.0 / (1.0 + jnp.exp(level[1] - level[0])),
        1.0 / (1.0 + jnp.exp(level[0] - level[1])),
    ]
    named = jnp.concatenate(picks, axis=0)
    at = jnp.arange(2 * count, dtype=jnp.int32)
    before = (at[:, None] > at[None, :]).astype(half)
    place = jnp.sum(dot_nn(before, named.astype(half)) * named, axis=1).astype(jnp.int32)
    target = jnp.concatenate([routes[:, 0], routes[:, 1]]) * slot_rows + place
    slots = jnp.arange(experts * slot_rows, dtype=jnp.int32)
    table = (target[:, None] == slots[None, :]).astype(half)
    upstream = cotangent.astype(single)
    row_cot = jnp.concatenate([(g * upstream).astype(half) for g in gates], axis=0)
    sent = jnp.concatenate(
        [
            dot_tn(table[:count] + table[count:], normed_two)
            .astype(half)
            .reshape(experts, slot_rows, width),
            dot_tn(table, row_cot).astype(half).reshape(experts, slot_rows, width),
        ],
        axis=1,
    )
    came = lax.all_to_all(sent, "expert", split_axis=0, concat_axis=0, tiled=True)
    arrived = came[:, :slot_rows].reshape(-1, width)
    arrived_cot = came[:, slot_rows:].reshape(-1, width)
    produced, row_part, in_part, out_part = expert_pass(arrived, arrived_cot, in_full, out_full)
    back = jnp.concatenate(
        [
            produced.reshape(experts, slot_rows, width),
            row_part.reshape(experts, slot_rows, width),
        ],
        axis=1,
    )
    back = lax.all_to_all(back, "expert", split_axis=0, concat_axis=0, tiled=True)
    in_sum = lax.psum_scatter(in_part, "dp", scatter_dimension=0, tiled=True)
    out_sum = lax.psum_scatter(out_part, "dp", scatter_dimension=0, tiled=True)
    combined = back[:, :slot_rows].reshape(-1, width)
    returned = back[:, slot_rows:].reshape(-1, width)
    outputs = [dot_nn(table[:count], combined), dot_nn(table[count:], combined)]
    block_out = (after_attn + gates[0] * outputs[0] + gates[1] * outputs[1]).astype(half)
    gate_diff = jnp.sum(upstream * (outputs[0] - outputs[1]), axis=1, keepdims=True)
    logit_grad = (gates[0] * gates[1] * gate_diff * (picks[0] - picks[1])).astype(half)
    router_grad = dot_tn(normed_two, logit_grad)
    normed_two_grad = dot_nn(table[:count] + table[count:], returned) + dot_nt(
        logit_grad, router_half
    )
    norm_two_grad = jnp.stack(
        [jnp.sum(normed_two_grad * xhat_two, axis=0), jnp.sum(normed_two_grad, axis=0)]
    )
    attn_grad = upstream + norm_backward_pass(normed_two_grad, xhat_two, inv_two, norms[6])
    layer_one_grad, norm_one_grad, mix_grad, project_grad = attention_backward(
        attn_grad, saved_one, norms[4], mix_half, project_half
    )
    after_a_grad, dense_grad, lead_two_grad = dense_backward(
        jnp.pad(layer_one_grad, extra), after_a, norms[2:4], up_pre, dense_full
    )
    after_a_grad = after_a_grad[:count]
    token_input_grad, lead_one_grad, lead_mix_grad, lead_project_grad = attention_backward(
        after_a_grad, saved_a, norms[0], lead_mix_half, lead_project_half
    )
    small_grad = jnp.concatenate(
        [
            jnp.concatenate([lead_one_grad, lead_two_grad, norm_one_grad, norm_two_grad], axis=0).T,
            router_grad,
        ],
        axis=1,
    )
    small_grad = jnp.pad(small_grad, ((0, 0), (0, 128 - small_grad.shape[1]))).astype(half)
    own_grad = jnp.concatenate(
        [lead_mix_grad, lead_project_grad, mix_grad, project_grad], axis=1
    ).astype(half)
    lead_mix_sum, lead_project_sum, mix_sum, project_sum, small_sum, dense_sum = scatter_grads(
        own_grad.reshape(4, 2, ROWS, -1),
        dense_grad.reshape(4, 2, ROWS, -1),
        small_grad.reshape(4, 2, ROWS, -1),
    )
    split = dense_sum.shape[1] // 2
    lead_up_sum = dense_sum[:, :split]
    lead_down_sum = dense_sum[:, split:].T
    turned = small_sum[:, :8].T
    norm, matrix = (norm_rate, 0.0), (matrix_rate, decay_rate)
    table = (
        (lead_norm_one, lead_norm_one_state, turned[0:2], norm),
        (lead_mix, lead_mix_state, lead_mix_sum, matrix),
        (lead_project, lead_project_state, lead_project_sum, matrix),
        (lead_norm_two, lead_norm_two_state, turned[2:4], norm),
        (lead_up, lead_up_state, lead_up_sum, matrix),
        (lead_down, lead_down_state, lead_down_sum, matrix),
        (norm_first, norm_first_state, turned[4:6], norm),
        (mix_weight, mix_state, mix_sum, matrix),
        (project_weight, project_state, project_sum, matrix),
        (norm_second, norm_second_state, turned[6:8], norm),
        (router_weight, router_state, small_sum[:, 8:24], matrix),
        (expert_in, expert_in_state, in_sum, matrix),
        (expert_out, expert_out_state, out_sum, matrix),
    )
    params, states, grads, rates = zip(*table)
    return (block_out, token_input_grad, *adam_all(params, states, grads, rates))


def solution(mesh):
    placed = (
        P(("dp", "expert"), None),
        P(("dp", "expert"), None),
        P(("dp", "expert"), None),
        P(None, ("dp", "expert")),
        P(None, None, ("dp", "expert")),
        P(("dp", "expert"), None),
        P(None, ("dp", "expert"), None),
        P(("dp", "expert"), None),
        P(None, ("dp", "expert"), None),
        P(None, ("dp", "expert")),
        P(None, None, ("dp", "expert")),
        P("dp", "expert"),
        P(None, "dp", "expert"),
        P("expert", "dp"),
        P(None, "expert", "dp"),
        P(None, ("dp", "expert")),
        P(None, None, ("dp", "expert")),
        P(("dp", "expert"), None),
        P(None, ("dp", "expert"), None),
        P(("dp", "expert"), None),
        P(None, ("dp", "expert"), None),
        P(None, ("dp", "expert")),
        P(None, None, ("dp", "expert")),
        P(("dp", "expert"), None),
        P(None, ("dp", "expert"), None),
        P("expert", None, "dp"),
        P(None, "expert", None, "dp"),
        P("expert", "dp", None),
        P(None, "expert", "dp", None),
    )
    return jax.shard_map(
        body,
        mesh=mesh,
        in_specs=placed,
        out_specs=(
            P(("dp", "expert"), None),
            P(("dp", "expert"), None),
            P(None, ("dp", "expert")),
            P(None, ("dp", "expert")),
            P(None, None, ("dp", "expert")),
            P(("dp", "expert"), None),
            P(("dp", "expert"), None),
            P(None, ("dp", "expert"), None),
            P(("dp", "expert"), None),
            P(("dp", "expert"), None),
            P(None, ("dp", "expert"), None),
            P(None, ("dp", "expert")),
            P(None, ("dp", "expert")),
            P(None, None, ("dp", "expert")),
            P("dp", "expert"),
            P("dp", "expert"),
            P(None, "dp", "expert"),
            P("expert", "dp"),
            P("expert", "dp"),
            P(None, "expert", "dp"),
            P(None, ("dp", "expert")),
            P(None, ("dp", "expert")),
            P(None, None, ("dp", "expert")),
            P(("dp", "expert"), None),
            P(("dp", "expert"), None),
            P(None, ("dp", "expert"), None),
            P(("dp", "expert"), None),
            P(("dp", "expert"), None),
            P(None, ("dp", "expert"), None),
            P(None, ("dp", "expert")),
            P(None, ("dp", "expert")),
            P(None, None, ("dp", "expert")),
            P(("dp", "expert"), None),
            P(("dp", "expert"), None),
            P(None, ("dp", "expert"), None),
            P("expert", None, "dp"),
            P("expert", None, "dp"),
            P(None, "expert", None, "dp"),
            P("expert", "dp", None),
            P("expert", "dp", None),
            P(None, "expert", "dp", None),
        ),
        check_vma=False,
    )
```

```python
import functools

import jax
import jax.numpy as jnp
from jax import lax
from jax.experimental import pallas as pl
from jax.experimental.pallas import tpu as pltpu
from jax.sharding import PartitionSpec as P

HEADS = 12
HEAD_DIM = 64
SEQ = 197
STEP = 3


norm_eps = 1e-06
beta_one = 0.9
beta_two = 0.999
adam_eps = 1e-08
matrix_rate = 0.03
norm_rate = 0.3
decay_rate = 0.05
root_half = 0.7071067811865476
inv_root_tau = 0.3989422804014327


def layer_normalize(rows):
    center = jnp.mean(rows, axis=-1, keepdims=True)
    offset = rows - center
    spread = jnp.mean(offset * offset, axis=-1, keepdims=True)
    inverse_stddev = lax.rsqrt(spread + norm_eps)
    return (offset * inverse_stddev, inverse_stddev)


def norm_backward_pass(upper_bound, centered_scaled, inverse_stddev, norm_gain):
    scaled_rows = upper_bound * norm_gain
    return inverse_stddev * (
        scaled_rows
        - jnp.mean(scaled_rows, axis=-1, keepdims=True)
        - centered_scaled * jnp.mean(scaled_rows * centered_scaled, axis=-1, keepdims=True)
    )


def dot_nn(a, b):
    return lax.dot_general(a, b, (((1,), (0,)), ((), ())), preferred_element_type=jnp.float32)


def dot_nt(a, b):
    return lax.dot_general(a, b, (((1,), (1,)), ((), ())), preferred_element_type=jnp.float32)


def dot_tn(a, b):
    return lax.dot_general(a, b, (((0,), (0,)), ((), ())), preferred_element_type=jnp.float32)


MESH = pl.DeviceIdType.MESH
BLK = 384
ROWS = 96
BIG = 3 * BLK - 256


def place():
    dp, e = lax.axis_index("dp"), lax.axis_index("expert")
    return dp, e, dp // 2, lax.rem(dp, 2), e // 4, lax.rem(e, 4)


def send(src, dst, send_sem, recv_sem, device):
    return pltpu.make_async_remote_copy(
        src_ref=src,
        dst_ref=dst,
        send_sem=send_sem,
        recv_sem=recv_sem,
        device_id=device,
        device_id_type=MESH,
    )


def meet():
    dp, e, z, c, _, _ = place()
    barrier = pltpu.get_barrier_semaphore()

    def greet(k, carry):
        pl.semaphore_signal(
            barrier, inc=1, device_id=(dp, lax.rem(e + k, 16)), device_id_type=MESH
        )
        return carry

    lax.fori_loop(1, 16, greet, 0)
    for k in range(1, 4):
        pl.semaphore_signal(
            barrier, inc=1, device_id=(2 * lax.rem(z + k, 4) + c, e), device_id_type=MESH
        )
    pl.semaphore_signal(barrier, inc=1, device_id=(2 * z + 1 - c, e), device_id_type=MESH)
    pl.semaphore_wait(barrier, 19)


def cell(path, first, second):
    _, _, _, _, y, x = place()
    dy, dx = (second, first) if path == 0 else (first, second)
    return lax.rem(y + dy, 4) * 4 + lax.rem(x + dx, 4)


def columns(block):
    return pl.ds(pl.multiple_of(block * BLK, BLK), BLK)


def swap_plane(source, target, send_sem, recv_sem):
    dp, e, _, _, _, _ = place()

    def one(k):
        peer = lax.rem(e + k, 16)
        return send(source.at[peer], target.at[e], send_sem.at[k], recv_sem.at[k], (dp, peer))

    def begin(k, carry):
        one(k).start()
        return carry

    def finish(k, carry):
        one(k).wait()
        return carry

    lax.fori_loop(1, 16, begin, 0)
    target[e] = source[e]
    lax.fori_loop(1, 16, finish, 0)


def six_of_eight(shape, row_dim):
    row = lax.broadcasted_iota(jnp.int32, shape, row_dim)
    col = lax.broadcasted_iota(jnp.int32, shape, 1 - row_dim)
    inner = jnp.bitwise_and(col, 7)
    same = (row == 6 * lax.shift_right_logical(col, 3) + inner) & (inner < 6)
    return jnp.where(same, 1.0, 0.0).astype(jnp.bfloat16)


def pieces(refs):
    lead_mix, lead_project, mix, project = refs
    for p in range(16):
        ref, at = ((lead_mix, 0), (lead_project, 6), (mix, 8), (project, 14))[
            0 if p < 6 else 1 if p < 8 else 2 if p < 14 else 3
        ]
        yield p, ref, slice((p - at) * BLK, (p - at + 1) * BLK)


def gather_kernel(
    lead_mix, lead_project, mix, project, small, dense,
    ga, gf, gs,
    wide, came, tower, s1, r1, s2, r2, s3, r3, s4, r4, local,
):
    dp, e, z, c, y, x = place()
    sibling = (2 * z + 1 - c, e)
    wide[...] = jnp.zeros_like(wide)
    for p, ref, cols in pieces((lead_mix, lead_project, mix, project)):
        wide[p, 0:6, 0:BLK] = ref[:, cols]
        wide[p, 0:6, BLK:512] = small[...]
    tower[z, :, 512:BIG] = dense[...]
    meet()

    def climb(path, k):
        part = tower.at[z, :, pl.ds(0, 512) if path == 0 else pl.ds(512, BLK)]
        return send(
            part, part, s2.at[path, k], r2.at[path, k], (2 * lax.rem(z + k, 4) + c, e)
        )

    for k in (1, 3, 2):
        climb(1, k).start()
    swap_plane(wide, came, s1, r1)
    rows = came[...].reshape(128, 512).astype(jnp.bfloat16)
    pick = six_of_eight((ROWS, 128), 0)
    tower[z, :, 0:512] = jnp.dot(pick, rows, preferred_element_type=jnp.float32).astype(
        jnp.bfloat16
    )
    for k in (1, 3, 2):
        climb(0, k).start()

    full, low, high = pl.ds(0, 4), pl.ds(0, 2), pl.ds(2, 2)
    whole = (ga, gf)
    start = (0, 512)

    def neighbour(path, axis, step):
        along_x = (axis == 0) == (path == 0)
        dx, dy = (step, 0) if along_x else (0, step)
        return (dp, lax.rem(y + dy, 4) * 4 + lax.rem(x + dx, 4))

    def at(path, first, second, part=full):
        return whole[path].at[part, c, :, columns(cell(path, first, second))]

    def own(path):
        return tower.at[:, :, pl.ds(start[path], BLK)]

    def move(path, number, device, first, second, part=full, source=None):
        ref = at(path, first, second, part)
        return send(
            ref if source is None else source, ref, s3.at[path, number], r3.at[path, number], device
        )

    slots = (0, 3, 1, 2)
    begun = []

    def go(*args, **named):
        copy = move(*args, **named)
        copy.start()
        begun.append(copy)

    def arrived(path, number, first, second, part=full):
        move(path, number, sibling, first, second, part).wait_recv()

    def spread(path, j, source=None):
        first = slots[j]
        go(path, 4 + 4 * j, neighbour(path, 1, 1), first, 0, source=source)
        go(path, 5 + 4 * j, neighbour(path, 1, 3), first, 0, source=source)
        go(path, 20 + 4 * j, sibling, first, 0, source=source)

    keep = []
    for path in (1, 0):
        for k in (1, 3, 2):
            climb(path, k).wait()
        go(path, 0, neighbour(path, 0, 1), 0, 0, source=own(path))
        go(path, 1, neighbour(path, 0, 3), 0, 0, source=own(path))
        spread(path, 0, source=own(path))
        copy = pltpu.make_async_copy(own(path), at(path, 0, 0), local.at[path])
        copy.start()
        keep.append(copy)
    minor = send(
        tower.at[:, :, pl.ds(BLK, 128)], gs.at[:, c], s4.at[0], r4.at[0], sibling
    )
    minor.start()
    copy = pltpu.make_async_copy(tower.at[:, :, pl.ds(BLK, 128)], gs.at[:, c], local.at[2])
    copy.start()
    keep.append(copy)
    for path in (1, 0):
        arrived(path, 0, 3, 0)
        go(path, 2, neighbour(path, 0, 1), 3, 0, low)
        arrived(path, 1, 1, 0)
        go(path, 3, neighbour(path, 0, 3), 1, 0, high)
    for path in (1, 0):
        spread(path, 1)
        spread(path, 2)
    for j in range(4):
        first = slots[j]
        if j == 1:
            for path in (1, 0):
                arrived(path, 2, 2, 0, low)
                arrived(path, 3, 2, 0, high)
                spread(path, 3)
        for path in (1, 0):
            arrived(path, 4 + 4 * j, first, 3)
            go(path, 6 + 4 * j, neighbour(path, 1, 1), first, 3, low)
            go(path, 21 + 4 * j, sibling, first, 3)
            arrived(path, 5 + 4 * j, first, 1)
            go(path, 7 + 4 * j, neighbour(path, 1, 3), first, 1, high)
            go(path, 22 + 4 * j, sibling, first, 1)
    for j in range(4):
        first = slots[j]
        for path in (1, 0):
            arrived(path, 6 + 4 * j, first, 2, low)
            arrived(path, 7 + 4 * j, first, 2, high)
            go(path, 23 + 4 * j, sibling, first, 2)
    for copy in keep:
        copy.wait()
    minor.wait()
    for copy in begun:
        copy.wait_send()
    for path in (0, 1):
        for number in range(20, 36):
            arrived(path, number, 0, 0)


def gather_weights(lead_mix, lead_project, mix, project, small, dense):
    half = jnp.bfloat16
    vmem = pl.BlockSpec(memory_space=pltpu.VMEM)
    hbm = pl.BlockSpec(memory_space=pl.ANY)
    dma = pltpu.SemaphoreType.DMA
    return pl.pallas_call(
        gather_kernel,
        out_shape=[
            jax.ShapeDtypeStruct((4, 2, ROWS, 16 * BLK), half),
            jax.ShapeDtypeStruct((4, 2, ROWS, 16 * BLK), half),
            jax.ShapeDtypeStruct((4, 2, ROWS, 128), half),
        ],
        in_specs=[vmem] * 6,
        out_specs=[hbm] * 3,
        scratch_shapes=[
            pltpu.VMEM((16, 8, 512), jnp.float32),
            pltpu.VMEM((16, 8, 512), jnp.float32),
            pltpu.VMEM((4, ROWS, BIG), half),
            dma((16,)), dma((16,)), dma((2, 4)), dma((2, 4)),
            dma((2, 36)), dma((2, 36)), dma((1,)), dma((1,)), dma((3,)),
        ],
        compiler_params=pltpu.CompilerParams(
            collective_id=0, has_side_effects=True, vmem_limit_bytes=60 * 2**20
        ),
    )(lead_mix, lead_project, mix, project, small, dense)


def scatter_kernel(
    da, df, ds,
    lead_mix, lead_project, mix, project, small, dense,
    acc, other, m1, m2, n1, n2, tower, layers, minor, wide, came,
    loc, ss, rs, t1, u1, t2, u2, v1, w1, v2, w2, s2, r2, s4, r4, s1, r1,
):
    single, half = jnp.float32, jnp.bfloat16
    dp, e, z, c, y, x = place()
    sibling = (2 * z + 1 - c, e)
    full, low, high = pl.ds(0, 4), pl.ds(0, 2), pl.ds(2, 2)
    parts = (da, df)
    order = (2, 1, 3, 0)

    def neighbour(path, axis, step):
        along_x = (axis == 0) == (path == 0)
        dx, dy = (step, 0) if along_x else (0, step)
        return (dp, lax.rem(y + dy, 4) * 4 + lax.rem(x + dx, 4))

    def block(path, first, second, part=full):
        return acc.at[path, part, :, columns(cell(path, first, second))]

    def load(path, first, second):
        cols = columns(cell(path, first, second))
        return pltpu.make_async_copy(
            parts[path].at[:, c, :, cols], acc.at[path, :, :, cols], loc.at[path, second, first]
        )

    def cross(path, first, second):
        cols = columns(cell(path, first, second))
        return send(
            parts[path].at[:, 1 - c, :, cols],
            other.at[path, :, :, cols],
            ss.at[path, second, first],
            rs.at[path, second, first],
            sibling,
        )

    loads = [(path, first, second) for second in order for path in (0, 1) for first in order]
    for spot in loads:
        load(*spot).start()
    meet()
    for spot in loads:
        cross(*spot).start()
    little = send(ds.at[:, 1 - c], minor.at[1], s4.at[0], r4.at[0], sibling)
    little.start()
    mine = pltpu.make_async_copy(ds.at[:, c], minor.at[0], s4.at[1])
    mine.start()

    def total(ref, *terms):
        value = ref[...]
        for term in terms:
            value = value + term[...]
        ref[...] = value

    def ready(path, first, second):
        load(path, first, second).wait()
        cross(path, first, second).wait()
        return other.at[path, :, :, columns(cell(path, first, second))]

    def far(path, first, up):
        return send(
            block(path, first, 2, low if up else high),
            m1.at[path, first, 0 if up else 1],
            t1.at[path, first, 0 if up else 1],
            u1.at[path, first, 0 if up else 1],
            neighbour(path, 1, 1 if up else 3),
        )

    def near(path, first, up):
        return send(
            block(path, first, 1 if up else 3),
            m2.at[path, first, 0 if up else 1],
            t2.at[path, first, 0 if up else 1],
            u2.at[path, first, 0 if up else 1],
            neighbour(path, 1, 1 if up else 3),
        )

    def last_far(path, up):
        return send(
            block(path, 2, 0, low if up else high),
            n1.at[path, 0 if up else 1],
            v1.at[path, 0 if up else 1],
            w1.at[path, 0 if up else 1],
            neighbour(path, 0, 1 if up else 3),
        )

    def last_near(path, up):
        return send(
            block(path, 1 if up else 3, 0),
            n2.at[path, 0 if up else 1],
            v2.at[path, 0 if up else 1],
            w2.at[path, 0 if up else 1],
            neighbour(path, 0, 1 if up else 3),
        )

    for path in (0, 1):
        for first in order:
            total(block(path, first, 2), ready(path, first, 2))
            far(path, first, True).start()
            far(path, first, False).start()
    for up in (True, False):
        second = 1 if up else 3
        for path in (0, 1):
            for first in order:
                term = ready(path, first, second)
                far(path, first, up).wait_recv()
                total(block(path, first, second), term)
                part = low if up else high
                total(block(path, first, second, part), m1.at[path, first, 0 if up else 1])
                near(path, first, up).start()
    for first in order:
        for path in (0, 1):
            term = ready(path, first, 0)
            near(path, first, True).wait_recv()
            near(path, first, False).wait_recv()
            total(block(path, first, 0), term, m2.at[path, first, 0], m2.at[path, first, 1])
            if first == 2:
                last_far(path, True).start()
                last_far(path, False).start()
            elif first != 0:
                up = first == 1
                last_far(path, up).wait_recv()
                part = low if up else high
                total(block(path, first, 0, part), n1.at[path, 0 if up else 1])
                last_near(path, up).start()
            else:
                last_near(path, True).wait_recv()
                last_near(path, False).wait_recv()
                total(block(path, 0, 0), n2.at[path, 0], n2.at[path, 1])
                lo = 0 if path == 0 else 512
                tower[:, :, lo : lo + BLK] = acc[path, :, :, columns(cell(path, 0, 0))]
    little.wait()
    mine.wait()
    tower[:, :, BLK:512] = (
        minor[0].astype(single) + minor[1].astype(single)
    ).astype(half)

    def fall(k):
        to = lax.rem(z + k, 4)
        return send(tower.at[to], layers.at[k], s2.at[k], r2.at[k], (2 * to + c, e))

    for k in (1, 3, 2):
        fall(k).start()
    value = tower[z].astype(single)
    for k in (1, 3, 2):
        fall(k).wait()
        value = value + layers[k].astype(single)
    dense[...] = value[:, 512:BIG]
    rows = value[:, 0:512]
    upper = rows.astype(half)
    lower = (rows - upper.astype(single)).astype(half)
    pick = six_of_eight((128, ROWS), 1)
    wide[...] = (
        jnp.dot(pick, upper, preferred_element_type=single)
        + jnp.dot(pick, lower, preferred_element_type=single)
    ).reshape(16, 8, 512)
    swap_plane(wide, came, s1, r1)
    for p, ref, cols in pieces((lead_mix, lead_project, mix, project)):
        ref[:, cols] = came[p, 0:6, 0:BLK]
    small[...] = jnp.sum(came[:, 0:6, BLK:512], axis=0)
    for path in (0, 1):
        for first in order:
            for up in (True, False):
                far(path, first, up).wait_send()
                near(path, first, up).wait_send()
        for up in (True, False):
            last_far(path, up).wait_send()
            last_near(path, up).wait_send()


def scatter_grads(da, df, ds):
    half, single = jnp.bfloat16, jnp.float32
    vmem = pl.BlockSpec(memory_space=pltpu.VMEM)
    hbm = pl.BlockSpec(memory_space=pl.ANY)
    dma = pltpu.SemaphoreType.DMA
    shape = jax.ShapeDtypeStruct
    return pl.pallas_call(
        scatter_kernel,
        out_shape=[
            shape((6, 2304), single), shape((6, 768), single),
            shape((6, 2304), single), shape((6, 768), single),
            shape((6, 128), single), shape((ROWS, BLK), single),
        ],
        in_specs=[hbm] * 3,
        out_specs=[vmem] * 6,
        scratch_shapes=[
            pltpu.VMEM((2, 4, ROWS, 16 * BLK), half),
            pltpu.VMEM((2, 4, ROWS, 16 * BLK), half),
            pltpu.VMEM((2, 4, 2, 2, ROWS, BLK), half),
            pltpu.VMEM((2, 4, 2, 4, ROWS, BLK), half),
            pltpu.VMEM((2, 2, 2, ROWS, BLK), half),
            pltpu.VMEM((2, 2, 4, ROWS, BLK), half),
            pltpu.VMEM((4, ROWS, BIG), half),
            pltpu.VMEM((4, ROWS, BIG), half),
            pltpu.VMEM((2, 4, ROWS, 128), half),
            pltpu.VMEM((16, 8, 512), single),
            pltpu.VMEM((16, 8, 512), single),
            dma((2, 4, 4)), dma((2, 4, 4)), dma((2, 4, 4)),
            dma((2, 4, 2)), dma((2, 4, 2)), dma((2, 4, 2)), dma((2, 4, 2)),
            dma((2, 2)), dma((2, 2)), dma((2, 2)), dma((2, 2)),
            dma((4,)), dma((4,)), dma((2,)), dma((2,)), dma((16,)), dma((16,)),
        ],
        compiler_params=pltpu.CompilerParams(
            collective_id=1, has_side_effects=True, vmem_limit_bytes=48 * 2**20
        ),
    )(da, df, ds)


PADDED = 208
GROUP = 4


def nn(a, b):
    return jnp.dot(a, b, preferred_element_type=jnp.float32)


def nt(a, b):
    return lax.dot_general(a, b, (((1,), (1,)), ((), ())), preferred_element_type=jnp.float32)


def tn(a, b):
    return lax.dot_general(a, b, (((0,), (0,)), ((), ())), preferred_element_type=jnp.float32)


def gelu_pair(pre):
    rise = 0.5 * (1.0 + lax.erf(pre * root_half))
    return pre * rise, rise + pre * jnp.exp(-0.5 * pre * pre) * inv_root_tau


def kept(value):
    lane = lax.broadcasted_iota(jnp.int32, value.shape, 1)
    return jnp.where(lane < BLK // 2, value, 0.0)


def dense_forward_kernel(rows, norm, both, out, hidden_out, slope_out, normed):
    half = jnp.bfloat16

    @pl.when(pl.program_id(0) == 0)
    def _():
        xhat, _ = layer_normalize(rows[...])
        normed[...] = (xhat * norm[0:1, :] + norm[1:2, :]).astype(half)
        out[...] = rows[...]

    total = jnp.zeros(out.shape, jnp.float32)
    for k in range(GROUP):
        at, to = k * BLK, k * 256
        value, slope = gelu_pair(nn(normed[...], both[:, at : at + 256]))
        slope_out[:, to : to + 256] = kept(slope)
        hidden = pltpu.roll(kept(value), 64, 1).astype(half)
        hidden_out[:, to : to + 256] = hidden
        total = total + nt(hidden, both[:, at + 128 : at + BLK])
    out[...] += total


def dense_backward_kernel(
    grad, rows, norm, hidden, slope, both, out, both_grad, norm_grad, low, normed_t, low_t, acc
):
    half, single = jnp.bfloat16, jnp.float32
    step = pl.program_id(0)

    @pl.when(step == 0)
    def _():
        xhat, _ = layer_normalize(rows[...])
        normed = (xhat * norm[0:1, :] + norm[1:2, :]).astype(half).astype(single)
        normed_t[...] = normed.T.astype(half)
        low[...] = grad[...].astype(half)
        low_t[...] = grad[...].T.astype(half)
        acc[...] = jnp.zeros_like(acc)

    total = jnp.zeros(acc.shape, single)
    for k in range(GROUP):
        at, to = k * BLK, k * 256
        hidden_grad = pltpu.roll(nn(low[...], both[:, at + 128 : at + BLK]), 192, 1)
        pre_grad = (hidden_grad * slope[:, to : to + 256]).astype(half)
        up = nn(normed_t[...], pre_grad)
        down = nn(low_t[...], hidden[:, to : to + 256])
        both_grad[:, at : at + 128] = up[:, 0:128].astype(half)
        both_grad[:, at + 128 : at + 256] = (up[:, 128:] + down[:, 0:128]).astype(half)
        both_grad[:, at + 256 : at + BLK] = down[:, 128:].astype(half)
        total = total + nt(pre_grad, both[:, at : at + 256])
    acc[...] += total

    @pl.when(step == pl.num_programs(0) - 1)
    def _():
        xhat, inverse = layer_normalize(rows[...])
        total = acc[...]
        norm_grad[0:1, :] = jnp.sum(total * xhat, axis=0, keepdims=True)
        norm_grad[1:2, :] = jnp.sum(total, axis=0, keepdims=True)
        out[...] = grad[...] + norm_backward_pass(total, xhat, inverse, norm[0:1, :])


def dense_forward(rows, norm, both):
    single, half = jnp.float32, jnp.bfloat16
    depth, wide = both.shape
    steps = wide // BLK
    shape = jax.ShapeDtypeStruct
    still = pl.BlockSpec((PADDED, depth), lambda i: (0, 0))
    moving = pl.BlockSpec((PADDED, GROUP * 256), lambda i: (0, i))
    return pl.pallas_call(
        dense_forward_kernel,
        grid=(steps // GROUP,),
        out_shape=[
            shape((PADDED, depth), single),
            shape((PADDED, steps * 256), half),
            shape((PADDED, steps * 256), single),
        ],
        in_specs=[
            still,
            pl.BlockSpec((2, depth), lambda i: (0, 0)),
            pl.BlockSpec((depth, GROUP * BLK), lambda i: (0, i)),
        ],
        out_specs=[still, moving, moving],
        scratch_shapes=[pltpu.VMEM((PADDED, depth), half)],
        compiler_params=pltpu.CompilerParams(vmem_limit_bytes=60 * 2**20),
    )(rows, norm, both)


def dense_backward(grad, rows, norm, hidden, slope, both):
    single, half = jnp.float32, jnp.bfloat16
    depth, wide = both.shape
    shape = jax.ShapeDtypeStruct
    still = pl.BlockSpec((PADDED, depth), lambda i: (0, 0))
    moving = pl.BlockSpec((PADDED, GROUP * 256), lambda i: (0, i))
    pair = pl.BlockSpec((2, depth), lambda i: (0, 0))
    block = pl.BlockSpec((depth, GROUP * BLK), lambda i: (0, i))
    return pl.pallas_call(
        dense_backward_kernel,
        grid=(wide // BLK // GROUP,),
        out_shape=[
            shape((PADDED, depth), single),
            shape((depth, wide), half),
            shape((2, depth), single),
        ],
        in_specs=[still, still, pair, moving, moving, block],
        out_specs=[still, block, pair],
        scratch_shapes=[
            pltpu.VMEM((PADDED, depth), half),
            pltpu.VMEM((depth, PADDED), half),
            pltpu.VMEM((depth, PADDED), half),
            pltpu.VMEM((PADDED, depth), single),
        ],
        compiler_params=pltpu.CompilerParams(vmem_limit_bytes=60 * 2**20),
    )(grad, rows, norm, hidden, slope, both)


def keys_bias():
    lane = lax.broadcasted_iota(jnp.int32, (PADDED, PADDED), 1)
    return jnp.where(lane < SEQ, 0.0, -1e30)


def of_head(value, h):
    lane = lax.broadcasted_iota(jnp.int32, value.shape, 1)
    mine = (lane < HEAD_DIM) if h == 0 else (lane >= HEAD_DIM)
    return jnp.where(mine, value, jnp.zeros_like(value))


def attention_forward_kernel(rows, norm, weights, out, mixed, context, lse):
    half, single = jnp.bfloat16, jnp.float32
    depth = rows.shape[1]
    xhat, _ = layer_normalize(rows[...])
    normed = (xhat * norm[0:1, :] + norm[1:2, :]).astype(half)
    mixed[:, 0:depth] = (nn(normed, weights[:, 0:depth]) * 0.125).astype(half)
    mixed[:, depth : 3 * depth] = nn(normed, weights[:, depth : 3 * depth]).astype(half)
    bias = keys_bias()
    lane = lax.broadcasted_iota(jnp.int32, (PADDED, 128), 1)
    totals = jnp.zeros((PADDED, 128), single)
    for pair in range(HEADS // 2):
        at = pair * 128
        query = mixed[:, at : at + 128]
        key = mixed[:, depth + at : depth + at + 128]
        value = mixed[:, 2 * depth + at : 2 * depth + at + 128]
        made = jnp.zeros((PADDED, 128), single)
        for h in range(2):
            scores = nt(of_head(query, h), key) + bias
            top = jnp.max(scores, axis=1, keepdims=True)
            total = top + jnp.log(jnp.sum(jnp.exp(scores - top), axis=1, keepdims=True))
            probs = jnp.exp(scores - total).astype(half)
            made = made + of_head(nn(probs, value), h)
            totals = jnp.where(lane == 2 * pair + h, total, totals)
        context[:, at : at + 128] = made.astype(half)
    lse[...] = totals
    out[...] = rows[...] + nn(context[...], weights[:, 3 * depth : 4 * depth])


def attention_backward_kernel(
    grad, rows, norm, weights, mixed, context, lse, kept_grads, out, norm_grad, both_grad, mixed_grad
):
    half, single = jnp.bfloat16, jnp.float32
    depth = rows.shape[1]
    xhat, inverse = layer_normalize(rows[...])
    normed_t = (xhat * norm[0:1, :] + norm[1:2, :]).astype(half).astype(single).T.astype(half)
    low = grad[...].astype(half)
    context_t = context[...].astype(single).T.astype(half)
    both_grad[:, 3 * depth : 4 * depth] = nn(context_t, low).astype(half)
    context_grad = nt(low, weights[:, 3 * depth : 4 * depth]).astype(half)
    bias = keys_bias()
    totals = lse[...]
    for pair in range(HEADS // 2):
        at = pair * 128
        query = mixed[:, at : at + 128]
        key = mixed[:, depth + at : depth + at + 128]
        value = mixed[:, 2 * depth + at : 2 * depth + at + 128]
        turn = context_grad[:, at : at + 128]
        zero = jnp.zeros((PADDED, 128), single)
        query_grad, key_grad, value_grad = zero, zero, zero
        for h in range(2):
            k = 2 * pair + h
            probs = jnp.exp(nt(of_head(query, h), key) + bias - totals[:, k : k + 1])
            value_grad = value_grad + of_head(tn(probs.astype(half), turn), h)
            prob_grad = nt(of_head(turn, h), value)
            inner = jnp.sum(probs * prob_grad, axis=1, keepdims=True)
            score_grad = (probs * (prob_grad - inner)).astype(half)
            query_grad = query_grad + of_head(nn(score_grad, key), h)
            key_grad = key_grad + of_head(tn(score_grad, query), h)
        mixed_grad[:, at : at + 128] = (query_grad * 0.125).astype(half)
        mixed_grad[:, depth + at : depth + at + 128] = key_grad.astype(half)
        mixed_grad[:, 2 * depth + at : 2 * depth + at + 128] = value_grad.astype(half)
    both_grad[:, 0 : 3 * depth] = nn(normed_t, mixed_grad[...]).astype(half)
    total = nt(mixed_grad[...], weights[:, 0 : 3 * depth])
    norm_grad[0:1, :] = jnp.sum(total * xhat, axis=0, keepdims=True)
    norm_grad[1:2, :] = jnp.sum(total, axis=0, keepdims=True)
    out[...] = grad[...] + norm_backward_pass(total, xhat, inverse, norm[0:1, :])


def whole_block(shape):
    return pl.BlockSpec(shape, lambda i: (0, 0))


def attention_forward(rows, norm, weights, which):
    half, single = jnp.bfloat16, jnp.float32
    count, depth = rows.shape
    shape = jax.ShapeDtypeStruct
    outs = [
        shape((count, depth), single),
        shape((count, 3 * depth), half),
        shape((count, depth), half),
        shape((count, 128), single),
    ]
    return pl.pallas_call(
        attention_forward_kernel,
        grid=(1,),
        out_shape=outs,
        in_specs=[
            whole_block(rows.shape),
            whole_block(norm.shape),
            pl.BlockSpec((depth, 4 * depth), lambda i: (0, which)),
        ],
        out_specs=[whole_block(o.shape) for o in outs],
        compiler_params=pltpu.CompilerParams(vmem_limit_bytes=48 * 2**20),
    )(rows, norm, weights)


def attention_backward(grad, rows, norm, weights, saved, which, filled):
    half, single = jnp.bfloat16, jnp.float32
    count, depth = rows.shape
    mixed, context, lse = saved
    shape = jax.ShapeDtypeStruct
    block = pl.BlockSpec((depth, 4 * depth), lambda i: (0, which))
    operands = [grad, rows, norm, weights, mixed, context, lse]
    in_specs = [
        whole_block(grad.shape), whole_block(rows.shape), whole_block(norm.shape), block,
        whole_block(mixed.shape), whole_block(context.shape), whole_block(lse.shape),
    ]
    if filled is None:
        body_kernel = lambda *refs: attention_backward_kernel(*refs[:7], None, *refs[7:])
        aliases = {}
    else:
        body_kernel = attention_backward_kernel
        operands.append(filled)
        in_specs.append(pl.BlockSpec(memory_space=pl.ANY))
        aliases = {7: 2}
    return pl.pallas_call(
        body_kernel,
        grid=(1,),
        out_shape=[
            shape((count, depth), single), shape((2, depth), single), shape(weights.shape, half)
        ],
        in_specs=in_specs,
        out_specs=[whole_block((count, depth)), whole_block((2, depth)), block],
        scratch_shapes=[pltpu.VMEM((count, 3 * depth), half)],
        input_output_aliases=aliases,
        compiler_params=pltpu.CompilerParams(vmem_limit_bytes=56 * 2**20),
    )(*operands)


SLOTS = 32


def expert_kernel(
    sent, w_in, w_out, home, in_grad, out_grad,
    came, ret, wi, wo, slope, hidden, pre_grad, acc, rows_t, cot_t, stage_in, stage_out,
    loads, stores, s1, r1, s2, r2,
):
    half, single = jnp.bfloat16, jnp.float32
    dp, e, _, _, _, _ = place()
    parts = wi.shape[0]
    rows_count = 16 * SLOTS
    depth = wi.shape[1]

    def fetch(b, k):
        source, target = ((w_in, wi), (w_out, wo))[k]
        return pltpu.make_async_copy(source.at[b], target.at[b], loads.at[b, k])

    def begin(b, carry):
        fetch(b, 0).start()
        fetch(b, 1).start()
        return carry

    lax.fori_loop(0, parts, begin, 0)
    barrier = pltpu.get_barrier_semaphore()

    def greet(k, carry):
        pl.semaphore_signal(
            barrier, inc=1, device_id=(dp, lax.rem(e + k, 16)), device_id_type=MESH
        )
        return carry

    lax.fori_loop(1, 16, greet, 0)
    pl.semaphore_wait(barrier, 15)

    def route(source, target, which, k, send_sem, recv_sem):
        peer = lax.rem(e + k, 16)
        cut = pl.ds(which * SLOTS, SLOTS)
        return send(
            source.at[peer, cut],
            target.at[e, cut],
            send_sem.at[which, k],
            recv_sem.at[which, k],
            (dp, peer),
        )

    def depart(source, target, which, send_sem, recv_sem):
        def one(k, carry):
            route(source, target, which, k, send_sem, recv_sem).start()
            return carry

        lax.fori_loop(1, 16, one, 0)

    def arrive(source, target, which, send_sem, recv_sem):
        def one(k, carry):
            route(source, target, which, k, send_sem, recv_sem).wait()
            return carry

        lax.fori_loop(1, 16, one, 0)

    depart(sent, came, 0, s1, r1)
    depart(sent, came, 1, s1, r1)
    came[e] = sent[e]
    arrive(sent, came, 0, s1, r1)
    rows = came[:, 0:SLOTS, :].reshape(rows_count, depth)
    acc[...] = jnp.zeros_like(acc)

    def forward(b, carry):
        fetch(b, 0).wait()
        fetch(b, 1).wait()
        value, rise = gelu_pair(nn(rows, wi[b]))
        slope[b] = rise
        mid = value.astype(half)
        hidden[b] = mid
        acc[...] += nn(mid, wo[b])
        return carry

    lax.fori_loop(0, parts, forward, 0)
    ret[:, 0:SLOTS, :] = acc[...].astype(half).reshape(16, SLOTS, depth)
    depart(ret, home, 0, s2, r2)
    rows_t[...] = rows.T
    arrive(sent, came, 1, s1, r1)
    cot = came[:, SLOTS:, :].reshape(rows_count, depth)
    acc[...] = jnp.zeros_like(acc)

    def backward(b, carry):
        grad = (nt(cot, wo[b]) * slope[b]).astype(half)
        pre_grad[b] = grad
        acc[...] += nt(grad, wi[b])
        return carry

    lax.fori_loop(0, parts, backward, 0)
    ret[:, SLOTS:, :] = acc[...].astype(half).reshape(16, SLOTS, depth)
    depart(ret, home, 1, s2, r2)
    home[e] = ret[e]
    cot_t[...] = cot.T

    def store(b, k):
        source, target = ((stage_in, in_grad), (stage_out, out_grad))[k]
        return pltpu.make_async_copy(source.at[b], target.at[b], stores.at[b, k])

    def weigh(b, carry):
        stage_in[b] = nn(rows_t[...], pre_grad[b]).astype(half)
        store(b, 0).start()
        stage_out[b] = nn(cot_t[...], hidden[b]).astype(half)
        store(b, 1).start()
        return carry

    lax.fori_loop(0, parts, weigh, 0)

    def settle(b, carry):
        store(b, 0).wait()
        store(b, 1).wait()
        return carry

    lax.fori_loop(0, parts, settle, 0)
    arrive(ret, home, 0, s2, r2)
    arrive(ret, home, 1, s2, r2)


def expert_pass(sent, w_in, w_out):
    half, single = jnp.bfloat16, jnp.float32
    parts, depth, inner = w_in.shape
    count = 16 * SLOTS
    shape = jax.ShapeDtypeStruct
    vmem = pl.BlockSpec(memory_space=pltpu.VMEM)
    hbm = pl.BlockSpec(memory_space=pl.ANY)
    dma = pltpu.SemaphoreType.DMA
    return pl.pallas_call(
        expert_kernel,
        out_shape=[shape(sent.shape, half), shape(w_in.shape, half), shape(w_in.shape, half)],
        in_specs=[vmem, hbm, hbm],
        out_specs=[vmem, hbm, hbm],
        scratch_shapes=[
            pltpu.VMEM(sent.shape, half),
            pltpu.VMEM(sent.shape, half),
            pltpu.VMEM(w_in.shape, half),
            pltpu.VMEM(w_out.shape, half),
            pltpu.VMEM((parts, count, inner), single),
            pltpu.VMEM((parts, count, inner), half),
            pltpu.VMEM((parts, count, inner), half),
            pltpu.VMEM((count, depth), single),
            pltpu.VMEM((depth, count), half),
            pltpu.VMEM((depth, count), half),
            pltpu.VMEM(w_in.shape, half),
            pltpu.VMEM(w_in.shape, half),
            dma((parts, 2)), dma((parts, 2)),
            dma((2, 16)), dma((2, 16)), dma((2, 16)), dma((2, 16)),
        ],
        compiler_params=pltpu.CompilerParams(
            collective_id=2, has_side_effects=True, vmem_limit_bytes=56 * 2**20
        ),
    )(sent, w_in, w_out)


def adam_kernel(rates, turned, *refs):
    count = len(rates)
    params, states, grads = refs[:count], refs[count : 2 * count], refs[2 * count : 3 * count]
    outs, scratch = refs[3 * count : 6 * count], refs[6 * count :]
    near, sems = scratch[:-1], scratch[-1]
    order = sorted(range(count), key=lambda k: -params[k].size)

    def load(k, which):
        source = (params, states, grads)[which][k]
        return pltpu.make_async_copy(source, near[3 * k + which], sems.at[0, 3 * k + which])

    def store(k, which):
        return pltpu.make_async_copy(
            near[3 * k + (2, 0, 1)[which]], outs[3 * k + which], sems.at[1, 3 * k + which]
        )

    wide = [k for k in range(count) if grads[k].dtype != jnp.float32]
    for k in order:
        load(k, 0).start()
        load(k, 1).start()
    for k in order:
        if k in wide:
            value = grads[k][0].astype(jnp.float32)
            near[3 * k + 2][0] = value if grads[k].shape == params[k].shape else value.T
        else:
            near[3 * k + 2][...] = grads[k][...]
        store(k, 0).start()
        load(k, 0).wait()
        load(k, 1).wait()
        grad, param, state = near[3 * k + 2][...], near[3 * k], near[3 * k + 1]
        rate, decay = rates[k]
        lower, upper = (slice(None), 0) if turned[k] else 0, (slice(None), 1) if turned[k] else 1
        first = beta_one * state[lower] + (1.0 - beta_one) * grad
        second = beta_two * state[upper] + (1.0 - beta_two) * grad * grad
        update = (
            first
            / (1.0 - beta_one**STEP)
            / (jnp.sqrt(second / (1.0 - beta_two**STEP)) + adam_eps)
        )
        param[...] = param[...] - rate * (update + decay * param[...])
        state[lower] = first
        state[upper] = second
        store(k, 1).start()
        store(k, 2).start()
    for k in order:
        for which in range(3):
            store(k, which).wait()


def adam_all(params, states, grads, rates):
    single = jnp.float32
    vmem = pl.BlockSpec(memory_space=pltpu.VMEM)
    hbm = pl.BlockSpec(memory_space=pl.ANY)
    shape = jax.ShapeDtypeStruct
    outs, near = [], []
    turned = [param.shape[0] == 6 for param in params]
    states = [s.swapaxes(0, 1) if t else s for s, t in zip(states, turned)]
    for param, state in zip(params, states):
        outs += [shape(param.shape, single), shape(param.shape, single), shape(state.shape, single)]
        near += [pltpu.VMEM(s.shape, single) for s in (param, state, param)]
    results = pl.pallas_call(
        functools.partial(adam_kernel, rates, turned),
        out_shape=outs,
        in_specs=[hbm] * (2 * len(params)) + [vmem] * len(params),
        out_specs=[hbm] * len(outs),
        scratch_shapes=[*near, pltpu.SemaphoreType.DMA((2, 3 * len(params)))],
        compiler_params=pltpu.CompilerParams(vmem_limit_bytes=56 * 2**20),
    )(*params, *states, *grads)
    results = list(results)
    for k, flip in enumerate(turned):
        if flip:
            results[3 * k + 2] = results[3 * k + 2].swapaxes(0, 1)
    return results


def body(
    tokens,
    routes,
    cotangent,
    lead_norm_one,
    lead_norm_one_state,
    lead_mix,
    lead_mix_state,
    lead_project,
    lead_project_state,
    lead_norm_two,
    lead_norm_two_state,
    lead_up,
    lead_up_state,
    lead_down,
    lead_down_state,
    norm_first,
    norm_first_state,
    mix_weight,
    mix_state,
    project_weight,
    project_state,
    norm_second,
    norm_second_state,
    router_weight,
    router_state,
    expert_in,
    expert_in_state,
    expert_out,
    expert_out_state,
):
    half = jnp.bfloat16
    single = jnp.float32
    count, width = tokens.shape
    experts = router_weight.shape[1]
    planes = lax.axis_size("expert")
    slot_rows = 32
    small = jnp.concatenate(
        [lead_norm_one.T, lead_norm_two.T, norm_first.T, norm_second.T, router_weight], axis=1
    )
    small = jnp.pad(small, ((0, 0), (0, 128 - small.shape[1])))
    dense = jnp.concatenate([lead_up, lead_down.T], axis=1).astype(half)
    own_full, dense_full, small_full = gather_weights(
        lead_mix, lead_project, mix_weight, project_weight, small, dense
    )
    own_full = own_full.reshape(width, -1)
    dense_full = dense_full.reshape(width, -1)
    small_full = small_full.reshape(width, -1)
    in_full = lax.all_gather(expert_in[0].astype(half), "dp", axis=0)
    out_full = lax.all_gather(expert_out[0].astype(half), "dp", axis=0)
    norms = small_full[:, :8].T.astype(single)
    router_half = small_full[:, 8:24]
    extra = ((0, PADDED - count), (0, 0))
    first_rows = jnp.pad(tokens.astype(single), extra)
    after_a, *saved_a = attention_forward(first_rows, norms[0:2], own_full, 0)
    layer_one, up_hidden, up_slope = dense_forward(after_a, norms[2:4], dense_full)
    after_attn, *saved_one = attention_forward(layer_one, norms[4:6], own_full, 1)
    after_attn = after_attn[:count]
    xhat_two, inv_two = layer_normalize(after_attn)
    normed_two = (xhat_two * norms[6] + norms[7]).astype(half)
    logits = dot_nn(normed_two, router_half)
    ids = jnp.arange(experts, dtype=jnp.int32)
    picks = [(routes[:, k : k + 1] == ids[None, :]).astype(single) for k in range(2)]
    level = [jnp.sum(p * logits, axis=1, keepdims=True) for p in picks]
    gates = [
        1.0 / (1.0 + jnp.exp(level[1] - level[0])),
        1.0 / (1.0 + jnp.exp(level[0] - level[1])),
    ]
    named = jnp.concatenate(picks, axis=0)
    at = jnp.arange(2 * count, dtype=jnp.int32)
    before = (at[:, None] > at[None, :]).astype(half)
    place = jnp.sum(dot_nn(before, named.astype(half)) * named, axis=1).astype(jnp.int32)
    target = jnp.concatenate([routes[:, 0], routes[:, 1]]) * slot_rows + place
    slots = jnp.arange(experts * slot_rows, dtype=jnp.int32)
    table = (target[:, None] == slots[None, :]).astype(half)
    upstream = cotangent.astype(single)
    row_cot = jnp.concatenate([(g * upstream).astype(half) for g in gates], axis=0)
    sent = jnp.concatenate(
        [
            dot_tn(table[:count] + table[count:], normed_two)
            .astype(half)
            .reshape(experts, slot_rows, width),
            dot_tn(table, row_cot).astype(half).reshape(experts, slot_rows, width),
        ],
        axis=1,
    )
    back, in_part, out_part = expert_pass(sent, in_full, out_full)
    in_sum = lax.psum_scatter(in_part, "dp", scatter_dimension=0, tiled=True)
    out_sum = lax.psum_scatter(out_part, "dp", scatter_dimension=0, tiled=True)
    combined = back[:, :slot_rows].reshape(-1, width)
    returned = back[:, slot_rows:].reshape(-1, width)
    outputs = [dot_nn(table[:count], combined), dot_nn(table[count:], combined)]
    block_out = (after_attn + gates[0] * outputs[0] + gates[1] * outputs[1]).astype(half)
    gate_diff = jnp.sum(upstream * (outputs[0] - outputs[1]), axis=1, keepdims=True)
    logit_grad = (gates[0] * gates[1] * gate_diff * (picks[0] - picks[1])).astype(half)
    router_grad = dot_tn(normed_two, logit_grad)
    normed_two_grad = dot_nn(table[:count] + table[count:], returned) + dot_nt(
        logit_grad, router_half
    )
    norm_two_grad = jnp.stack(
        [jnp.sum(normed_two_grad * xhat_two, axis=0), jnp.sum(normed_two_grad, axis=0)]
    )
    attn_grad = upstream + norm_backward_pass(normed_two_grad, xhat_two, inv_two, norms[6])
    layer_one_grad, norm_one_grad, own_grad = attention_backward(
        jnp.pad(attn_grad, extra), layer_one, norms[4:6], own_full, saved_one, 1, None
    )
    after_a_grad, dense_grad, lead_two_grad = dense_backward(
        layer_one_grad, after_a, norms[2:4], up_hidden, up_slope, dense_full
    )
    token_input_grad, lead_one_grad, own_grad = attention_backward(
        after_a_grad, first_rows, norms[0:2], own_full, saved_a, 0, own_grad
    )
    token_input_grad = token_input_grad[:count]
    small_grad = jnp.concatenate(
        [
            jnp.concatenate([lead_one_grad, lead_two_grad, norm_one_grad, norm_two_grad], axis=0).T,
            router_grad,
        ],
        axis=1,
    )
    small_grad = jnp.pad(small_grad, ((0, 0), (0, 128 - small_grad.shape[1]))).astype(half)
    lead_mix_sum, lead_project_sum, mix_sum, project_sum, small_sum, dense_sum = scatter_grads(
        own_grad.reshape(4, 2, ROWS, -1),
        dense_grad.reshape(4, 2, ROWS, -1),
        small_grad.reshape(4, 2, ROWS, -1),
    )
    split = dense_sum.shape[1] // 2
    lead_up_sum = dense_sum[:, :split]
    lead_down_sum = dense_sum[:, split:].T
    turned = small_sum[:, :8].T
    norm, matrix = (norm_rate, 0.0), (matrix_rate, decay_rate)
    table = (
        (lead_norm_one, lead_norm_one_state, turned[0:2], norm),
        (lead_mix, lead_mix_state, lead_mix_sum, matrix),
        (lead_project, lead_project_state, lead_project_sum, matrix),
        (lead_norm_two, lead_norm_two_state, turned[2:4], norm),
        (lead_up, lead_up_state, lead_up_sum, matrix),
        (lead_down, lead_down_state, lead_down_sum, matrix),
        (norm_first, norm_first_state, turned[4:6], norm),
        (mix_weight, mix_state, mix_sum, matrix),
        (project_weight, project_state, project_sum, matrix),
        (norm_second, norm_second_state, turned[6:8], norm),
        (router_weight, router_state, small_sum[:, 8:24], matrix),
        (expert_in, expert_in_state, in_sum, matrix),
        (expert_out, expert_out_state, out_sum, matrix),
    )
    params, states, grads, rates = zip(*table)
    return (block_out, token_input_grad, *adam_all(params, states, grads, rates))


def solution(mesh):
    placed = (
        P(("dp", "expert"), None),
        P(("dp", "expert"), None),
        P(("dp", "expert"), None),
        P(None, ("dp", "expert")),
        P(None, None, ("dp", "expert")),
        P(("dp", "expert"), None),
        P(None, ("dp", "expert"), None),
        P(("dp", "expert"), None),
        P(None, ("dp", "expert"), None),
        P(None, ("dp", "expert")),
        P(None, None, ("dp", "expert")),
        P("dp", "expert"),
        P(None, "dp", "expert"),
        P("expert", "dp"),
        P(None, "expert", "dp"),
        P(None, ("dp", "expert")),
        P(None, None, ("dp", "expert")),
        P(("dp", "expert"), None),
        P(None, ("dp", "expert"), None),
        P(("dp", "expert"), None),
        P(None, ("dp", "expert"), None),
        P(None, ("dp", "expert")),
        P(None, None, ("dp", "expert")),
        P(("dp", "expert"), None),
        P(None, ("dp", "expert"), None),
        P("expert", None, "dp"),
        P(None, "expert", None, "dp"),
        P("expert", "dp", None),
        P(None, "expert", "dp", None),
    )
    return jax.shard_map(
        body,
        mesh=mesh,
        in_specs=placed,
        out_specs=(
            P(("dp", "expert"), None),
            P(("dp", "expert"), None),
            P(None, ("dp", "expert")),
            P(None, ("dp", "expert")),
            P(None, None, ("dp", "expert")),
            P(("dp", "expert"), None),
            P(("dp", "expert"), None),
            P(None, ("dp", "expert"), None),
            P(("dp", "expert"), None),
            P(("dp", "expert"), None),
            P(None, ("dp", "expert"), None),
            P(None, ("dp", "expert")),
            P(None, ("dp", "expert")),
            P(None, None, ("dp", "expert")),
            P("dp", "expert"),
            P("dp", "expert"),
            P(None, "dp", "expert"),
            P("expert", "dp"),
            P("expert", "dp"),
            P(None, "expert", "dp"),
            P(None, ("dp", "expert")),
            P(None, ("dp", "expert")),
            P(None, None, ("dp", "expert")),
            P(("dp", "expert"), None),
            P(("dp", "expert"), None),
            P(None, ("dp", "expert"), None),
            P(("dp", "expert"), None),
            P(("dp", "expert"), None),
            P(None, ("dp", "expert"), None),
            P(None, ("dp", "expert")),
            P(None, ("dp", "expert")),
            P(None, None, ("dp", "expert")),
            P(("dp", "expert"), None),
            P(("dp", "expert"), None),
            P(None, ("dp", "expert"), None),
            P("expert", None, "dp"),
            P("expert", None, "dp"),
            P(None, "expert", None, "dp"),
            P("expert", "dp", None),
            P("expert", "dp", None),
            P(None, "expert", "dp", None),
        ),
        check_vma=False,
    )
```

```python
import functools

import jax
import jax.numpy as jnp
from jax import lax
from jax.experimental import pallas as pl
from jax.experimental.pallas import tpu as pltpu
from jax.sharding import PartitionSpec as P

HEADS = 12
HEAD_DIM = 64
SEQ = 197
STEP = 3


norm_eps = 1e-06
beta_one = 0.9
beta_two = 0.999
adam_eps = 1e-08
matrix_rate = 0.03
norm_rate = 0.3
decay_rate = 0.05
root_half = 0.7071067811865476
inv_root_tau = 0.3989422804014327


def layer_normalize(rows):
    center = jnp.mean(rows, axis=-1, keepdims=True)
    offset = rows - center
    spread = jnp.mean(offset * offset, axis=-1, keepdims=True)
    inverse_stddev = lax.rsqrt(spread + norm_eps)
    return (offset * inverse_stddev, inverse_stddev)


def norm_backward_pass(upper_bound, centered_scaled, inverse_stddev, norm_gain):
    scaled_rows = upper_bound * norm_gain
    return inverse_stddev * (
        scaled_rows
        - jnp.mean(scaled_rows, axis=-1, keepdims=True)
        - centered_scaled * jnp.mean(scaled_rows * centered_scaled, axis=-1, keepdims=True)
    )


def dot_nn(a, b):
    return lax.dot_general(a, b, (((1,), (0,)), ((), ())), preferred_element_type=jnp.float32)


def dot_nt(a, b):
    return lax.dot_general(a, b, (((1,), (1,)), ((), ())), preferred_element_type=jnp.float32)


def dot_tn(a, b):
    return lax.dot_general(a, b, (((0,), (0,)), ((), ())), preferred_element_type=jnp.float32)


MESH = pl.DeviceIdType.MESH
BLK = 384
ROWS = 96
BIG = 3 * BLK - 256


def place():
    dp, e = lax.axis_index("dp"), lax.axis_index("expert")
    return dp, e, dp // 2, lax.rem(dp, 2), e // 4, lax.rem(e, 4)


def send(src, dst, send_sem, recv_sem, device):
    return pltpu.make_async_remote_copy(
        src_ref=src,
        dst_ref=dst,
        send_sem=send_sem,
        recv_sem=recv_sem,
        device_id=device,
        device_id_type=MESH,
    )


def meet():
    dp, e, z, c, _, _ = place()
    barrier = pltpu.get_barrier_semaphore()

    def greet(k, carry):
        pl.semaphore_signal(
            barrier, inc=1, device_id=(dp, lax.rem(e + k, 16)), device_id_type=MESH
        )
        return carry

    lax.fori_loop(1, 16, greet, 0)
    for k in range(1, 4):
        pl.semaphore_signal(
            barrier, inc=1, device_id=(2 * lax.rem(z + k, 4) + c, e), device_id_type=MESH
        )
    pl.semaphore_signal(barrier, inc=1, device_id=(2 * z + 1 - c, e), device_id_type=MESH)
    pl.semaphore_wait(barrier, 19)


def cell(path, first, second):
    _, _, _, _, y, x = place()
    dy, dx = (second, first) if path == 0 else (first, second)
    return lax.rem(y + dy, 4) * 4 + lax.rem(x + dx, 4)


def columns(block):
    return pl.ds(pl.multiple_of(block * BLK, BLK), BLK)


def swap_step(source, target, send_sem, recv_sem, k):
    dp, e, _, _, _, _ = place()
    peer = lax.rem(e + k, 16)
    return send(source.at[peer], target.at[e], send_sem.at[k], recv_sem.at[k], (dp, peer))


def swap_plane_begin(source, target, send_sem, recv_sem):
    e = lax.axis_index("expert")

    def begin(k, carry):
        swap_step(source, target, send_sem, recv_sem, k).start()
        return carry

    lax.fori_loop(1, 16, begin, 0)
    target[e] = source[e]


def swap_plane_end(source, target, send_sem, recv_sem):
    def finish(k, carry):
        swap_step(source, target, send_sem, recv_sem, k).wait()
        return carry

    lax.fori_loop(1, 16, finish, 0)


def six_of_eight(shape, row_dim):
    row = lax.broadcasted_iota(jnp.int32, shape, row_dim)
    col = lax.broadcasted_iota(jnp.int32, shape, 1 - row_dim)
    inner = jnp.bitwise_and(col, 7)
    same = (row == 6 * lax.shift_right_logical(col, 3) + inner) & (inner < 6)
    return jnp.where(same, 1.0, 0.0).astype(jnp.bfloat16)


def pieces(refs):
    lead_mix, lead_project, mix, project = refs
    for p in range(16):
        ref, at = ((lead_mix, 0), (lead_project, 6), (mix, 8), (project, 14))[
            0 if p < 6 else 1 if p < 8 else 2 if p < 14 else 3
        ]
        yield p, ref, slice((p - at) * BLK, (p - at + 1) * BLK)


def gather_kernel(
    lead_mix, lead_project, mix, project, small, dense,
    ga, gf, gs,
    wide, came, tower, s1, r1, s2, r2, s3, r3, s4, r4, local,
):
    dp, e, z, c, y, x = place()
    sibling = (2 * z + 1 - c, e)
    wide[...] = jnp.zeros_like(wide)
    for p, ref, cols in pieces((lead_mix, lead_project, mix, project)):
        wide[p, 0:6, 0:BLK] = ref[:, cols]
        wide[p, 0:6, BLK:512] = small[...]
    tower[z, :, 512:BIG] = dense[...]
    meet()

    def climb(path, k):
        part = tower.at[z, :, pl.ds(0, 512) if path == 0 else pl.ds(512, BLK)]
        return send(
            part, part, s2.at[path, k], r2.at[path, k], (2 * lax.rem(z + k, 4) + c, e)
        )

    for k in (1, 3, 2):
        climb(1, k).start()
    swap_plane_begin(wide, came, s1, r1)
    swap_plane_end(wide, came, s1, r1)
    rows = came[...].reshape(128, 512).astype(jnp.bfloat16)
    pick = six_of_eight((ROWS, 128), 0)
    tower[z, :, 0:512] = jnp.dot(pick, rows, preferred_element_type=jnp.float32).astype(
        jnp.bfloat16
    )
    for k in (1, 3, 2):
        climb(0, k).start()

    full, low, high = pl.ds(0, 4), pl.ds(0, 2), pl.ds(2, 2)
    whole = (ga, gf)
    start = (0, 512)

    def neighbour(path, axis, step):
        along_x = (axis == 0) == (path == 0)
        dx, dy = (step, 0) if along_x else (0, step)
        return (dp, lax.rem(y + dy, 4) * 4 + lax.rem(x + dx, 4))

    def at(path, first, second, part=full):
        return whole[path].at[part, c, :, columns(cell(path, first, second))]

    def own(path):
        return tower.at[:, :, pl.ds(start[path], BLK)]

    def move(path, number, device, first, second, part=full, source=None):
        ref = at(path, first, second, part)
        return send(
            ref if source is None else source, ref, s3.at[path, number], r3.at[path, number], device
        )

    slots = (0, 3, 1, 2)
    begun = []

    def go(*args, **named):
        copy = move(*args, **named)
        copy.start()
        begun.append(copy)

    def arrived(path, number, first, second, part=full):
        move(path, number, sibling, first, second, part).wait_recv()

    def spread(path, j, source=None):
        first = slots[j]
        go(path, 4 + 4 * j, neighbour(path, 1, 1), first, 0, source=source)
        go(path, 5 + 4 * j, neighbour(path, 1, 3), first, 0, source=source)
        go(path, 20 + 4 * j, sibling, first, 0, source=source)

    keep = []
    for path in (1, 0):
        for k in (1, 3, 2):
            climb(path, k).wait()
        go(path, 0, neighbour(path, 0, 1), 0, 0, source=own(path))
        go(path, 1, neighbour(path, 0, 3), 0, 0, source=own(path))
        spread(path, 0, source=own(path))
        copy = pltpu.make_async_copy(own(path), at(path, 0, 0), local.at[path])
        copy.start()
        keep.append(copy)
    minor = send(
        tower.at[:, :, pl.ds(BLK, 128)], gs.at[:, c], s4.at[0], r4.at[0], sibling
    )
    minor.start()
    copy = pltpu.make_async_copy(tower.at[:, :, pl.ds(BLK, 128)], gs.at[:, c], local.at[2])
    copy.start()
    keep.append(copy)
    for path in (1, 0):
        arrived(path, 0, 3, 0)
        go(path, 2, neighbour(path, 0, 1), 3, 0, low)
        arrived(path, 1, 1, 0)
        go(path, 3, neighbour(path, 0, 3), 1, 0, high)
    for path in (1, 0):
        spread(path, 1)
        spread(path, 2)
    for j in range(4):
        first = slots[j]
        if j == 1:
            for path in (1, 0):
                arrived(path, 2, 2, 0, low)
                arrived(path, 3, 2, 0, high)
                spread(path, 3)
        for path in (1, 0):
            arrived(path, 4 + 4 * j, first, 3)
            go(path, 6 + 4 * j, neighbour(path, 1, 1), first, 3, low)
            go(path, 21 + 4 * j, sibling, first, 3)
            arrived(path, 5 + 4 * j, first, 1)
            go(path, 7 + 4 * j, neighbour(path, 1, 3), first, 1, high)
            go(path, 22 + 4 * j, sibling, first, 1)
    for j in range(4):
        first = slots[j]
        for path in (1, 0):
            arrived(path, 6 + 4 * j, first, 2, low)
            arrived(path, 7 + 4 * j, first, 2, high)
            go(path, 23 + 4 * j, sibling, first, 2)
    for copy in keep:
        copy.wait()
    minor.wait()
    for copy in begun:
        copy.wait_send()
    for path in (0, 1):
        for number in range(20, 36):
            arrived(path, number, 0, 0)


def gather_weights(lead_mix, lead_project, mix, project, small, dense):
    half = jnp.bfloat16
    vmem = pl.BlockSpec(memory_space=pltpu.VMEM)
    hbm = pl.BlockSpec(memory_space=pl.ANY)
    dma = pltpu.SemaphoreType.DMA
    return pl.pallas_call(
        gather_kernel,
        out_shape=[
            jax.ShapeDtypeStruct((4, 2, ROWS, 16 * BLK), half),
            jax.ShapeDtypeStruct((4, 2, ROWS, 16 * BLK), half),
            jax.ShapeDtypeStruct((4, 2, ROWS, 128), half),
        ],
        in_specs=[vmem] * 6,
        out_specs=[hbm] * 3,
        scratch_shapes=[
            pltpu.VMEM((16, 8, 512), jnp.float32),
            pltpu.VMEM((16, 8, 512), jnp.float32),
            pltpu.VMEM((4, ROWS, BIG), half),
            dma((16,)), dma((16,)), dma((2, 4)), dma((2, 4)),
            dma((2, 36)), dma((2, 36)), dma((1,)), dma((1,)), dma((3,)),
        ],
        compiler_params=pltpu.CompilerParams(
            collective_id=0, has_side_effects=True, vmem_limit_bytes=56 * 2**20
        ),
    )(lead_mix, lead_project, mix, project, small, dense)


def scatter_kernel(
    da, df, ds,
    lead_mix, lead_project, mix, project, small, dense,
    acc, other, m1, m2, n1, n2, tower, layers, minor, wide, came,
    loc, ss, rs, t1, u1, t2, u2, v1, w1, v2, w2, s2, r2, s4, r4, s1, r1,
):
    single, half = jnp.float32, jnp.bfloat16
    dp, e, z, c, y, x = place()
    sibling = (2 * z + 1 - c, e)
    full, low, high = pl.ds(0, 4), pl.ds(0, 2), pl.ds(2, 2)
    parts = (da, df)
    order = (2, 1, 3, 0)

    def neighbour(path, axis, step):
        along_x = (axis == 0) == (path == 0)
        dx, dy = (step, 0) if along_x else (0, step)
        return (dp, lax.rem(y + dy, 4) * 4 + lax.rem(x + dx, 4))

    def block(path, first, second, part=full):
        return acc.at[path, part, :, columns(cell(path, first, second))]

    def load(path, first, second):
        cols = columns(cell(path, first, second))
        return pltpu.make_async_copy(
            parts[path].at[:, c, :, cols], acc.at[path, :, :, cols], loc.at[path, second, first]
        )

    def cross(path, first, second):
        cols = columns(cell(path, first, second))
        return send(
            parts[path].at[:, 1 - c, :, cols],
            other.at[path, :, :, cols],
            ss.at[path, second, first],
            rs.at[path, second, first],
            sibling,
        )

    loads = [(path, first, second) for second in order for path in (0, 1) for first in order]
    for spot in loads:
        load(*spot).start()
    meet()
    for spot in loads:
        cross(*spot).start()
    little = send(ds.at[:, 1 - c], minor.at[1], s4.at[0], r4.at[0], sibling)
    little.start()
    mine = pltpu.make_async_copy(ds.at[:, c], minor.at[0], s4.at[1])
    mine.start()

    def total(ref, *terms):
        value = ref[...]
        for term in terms:
            value = value + term[...]
        ref[...] = value

    def ready(path, first, second):
        load(path, first, second).wait()
        cross(path, first, second).wait()
        return other.at[path, :, :, columns(cell(path, first, second))]

    def far(path, first, up):
        return send(
            block(path, first, 2, low if up else high),
            m1.at[path, first, 0 if up else 1],
            t1.at[path, first, 0 if up else 1],
            u1.at[path, first, 0 if up else 1],
            neighbour(path, 1, 1 if up else 3),
        )

    def near(path, first, up):
        return send(
            block(path, first, 1 if up else 3),
            m2.at[path, first, 0 if up else 1],
            t2.at[path, first, 0 if up else 1],
            u2.at[path, first, 0 if up else 1],
            neighbour(path, 1, 1 if up else 3),
        )

    def last_far(path, up):
        return send(
            block(path, 2, 0, low if up else high),
            n1.at[path, 0 if up else 1],
            v1.at[path, 0 if up else 1],
            w1.at[path, 0 if up else 1],
            neighbour(path, 0, 1 if up else 3),
        )

    def last_near(path, up):
        return send(
            block(path, 1 if up else 3, 0),
            n2.at[path, 0 if up else 1],
            v2.at[path, 0 if up else 1],
            w2.at[path, 0 if up else 1],
            neighbour(path, 0, 1 if up else 3),
        )

    def fall(path, k):
        to = lax.rem(z + k, 4)
        cols = pl.ds(0, 512) if path == 0 else pl.ds(512, BLK)
        return send(
            tower.at[to, :, cols],
            layers.at[k, :, cols],
            s2.at[path, k],
            r2.at[path, k],
            (2 * to + c, e),
        )

    for path in (0, 1):
        for first in order:
            total(block(path, first, 2), ready(path, first, 2))
            far(path, first, True).start()
            far(path, first, False).start()
    for up in (True, False):
        second = 1 if up else 3
        for path in (0, 1):
            for first in order:
                term = ready(path, first, second)
                far(path, first, up).wait_recv()
                total(block(path, first, second), term)
                part = low if up else high
                total(block(path, first, second, part), m1.at[path, first, 0 if up else 1])
                near(path, first, up).start()
    for first in order:
        for path in (0, 1):
            term = ready(path, first, 0)
            near(path, first, True).wait_recv()
            near(path, first, False).wait_recv()
            total(block(path, first, 0), term, m2.at[path, first, 0], m2.at[path, first, 1])
            if first == 2:
                last_far(path, True).start()
                last_far(path, False).start()
            elif first != 0:
                up = first == 1
                last_far(path, up).wait_recv()
                part = low if up else high
                total(block(path, first, 0, part), n1.at[path, 0 if up else 1])
                last_near(path, up).start()
            else:
                last_near(path, True).wait_recv()
                last_near(path, False).wait_recv()
                total(block(path, 0, 0), n2.at[path, 0], n2.at[path, 1])
                lo = 0 if path == 0 else 512
                tower[:, :, lo : lo + BLK] = acc[path, :, :, columns(cell(path, 0, 0))]
                if path == 0:
                    little.wait()
                    mine.wait()
                    tower[:, :, BLK:512] = (
                        minor[0].astype(single) + minor[1].astype(single)
                    ).astype(half)
                for k in (1, 3, 2):
                    fall(path, k).start()

    rows = tower[z, :, 0:512].astype(single)
    for k in (1, 3, 2):
        fall(0, k).wait()
        rows = rows + layers[k, :, 0:512].astype(single)
    upper = rows.astype(half)
    lower = (rows - upper.astype(single)).astype(half)
    pick = six_of_eight((128, ROWS), 1)
    wide[...] = (
        jnp.dot(pick, upper, preferred_element_type=single)
        + jnp.dot(pick, lower, preferred_element_type=single)
    ).reshape(16, 8, 512)
    swap_plane_begin(wide, came, s1, r1)
    value = tower[z, :, 512:BIG].astype(single)
    for k in (1, 3, 2):
        fall(1, k).wait()
        value = value + layers[k, :, 512:BIG].astype(single)
    dense[...] = value
    swap_plane_end(wide, came, s1, r1)
    for p, ref, cols in pieces((lead_mix, lead_project, mix, project)):
        ref[:, cols] = came[p, 0:6, 0:BLK]
    small[...] = jnp.sum(came[:, 0:6, BLK:512], axis=0)
    for path in (0, 1):
        for first in order:
            for up in (True, False):
                far(path, first, up).wait_send()
                near(path, first, up).wait_send()
        for up in (True, False):
            last_far(path, up).wait_send()
            last_near(path, up).wait_send()


def scatter_grads(da, df, ds):
    half, single = jnp.bfloat16, jnp.float32
    vmem = pl.BlockSpec(memory_space=pltpu.VMEM)
    hbm = pl.BlockSpec(memory_space=pl.ANY)
    dma = pltpu.SemaphoreType.DMA
    shape = jax.ShapeDtypeStruct
    return pl.pallas_call(
        scatter_kernel,
        out_shape=[
            shape((6, 2304), single), shape((6, 768), single),
            shape((6, 2304), single), shape((6, 768), single),
            shape((6, 128), single), shape((ROWS, BLK), single),
        ],
        in_specs=[hbm] * 3,
        out_specs=[vmem] * 6,
        scratch_shapes=[
            pltpu.VMEM((2, 4, ROWS, 16 * BLK), half),
            pltpu.VMEM((2, 4, ROWS, 16 * BLK), half),
            pltpu.VMEM((2, 4, 2, 2, ROWS, BLK), half),
            pltpu.VMEM((2, 4, 2, 4, ROWS, BLK), half),
            pltpu.VMEM((2, 2, 2, ROWS, BLK), half),
            pltpu.VMEM((2, 2, 4, ROWS, BLK), half),
            pltpu.VMEM((4, ROWS, BIG), half),
            pltpu.VMEM((4, ROWS, BIG), half),
            pltpu.VMEM((2, 4, ROWS, 128), half),
            pltpu.VMEM((16, 8, 512), single),
            pltpu.VMEM((16, 8, 512), single),
            dma((2, 4, 4)), dma((2, 4, 4)), dma((2, 4, 4)),
            dma((2, 4, 2)), dma((2, 4, 2)), dma((2, 4, 2)), dma((2, 4, 2)),
            dma((2, 2)), dma((2, 2)), dma((2, 2)), dma((2, 2)),
            dma((2, 4)), dma((2, 4)), dma((2,)), dma((2,)), dma((16,)), dma((16,)),
        ],
        compiler_params=pltpu.CompilerParams(
            collective_id=1, has_side_effects=True, vmem_limit_bytes=48 * 2**20
        ),
    )(da, df, ds)


PADDED = 208
GROUP = 4


def nn(a, b):
    return jnp.dot(a, b, preferred_element_type=jnp.float32)


def nt(a, b):
    return lax.dot_general(a, b, (((1,), (1,)), ((), ())), preferred_element_type=jnp.float32)


def tn(a, b):
    return lax.dot_general(a, b, (((0,), (0,)), ((), ())), preferred_element_type=jnp.float32)


def gelu_pair(pre):
    rise = 0.5 * (1.0 + lax.erf(pre * root_half))
    return pre * rise, rise + pre * jnp.exp(-0.5 * pre * pre) * inv_root_tau


def kept(value):
    lane = lax.broadcasted_iota(jnp.int32, value.shape, 1)
    return jnp.where(lane < BLK // 2, value, 0.0)


def dense_forward_kernel(rows, norm, both, out, hidden_out, slope_out, normed):
    half = jnp.bfloat16

    @pl.when(pl.program_id(0) == 0)
    def _():
        xhat, _ = layer_normalize(rows[...])
        normed[...] = (xhat * norm[0:1, :] + norm[1:2, :]).astype(half)
        out[...] = rows[...]

    total = jnp.zeros(out.shape, jnp.float32)
    for k in range(GROUP):
        at, to = k * BLK, k * 256
        value, slope = gelu_pair(nn(normed[...], both[:, at : at + 256]))
        slope_out[:, to : to + 256] = kept(slope)
        hidden = pltpu.roll(kept(value), 64, 1).astype(half)
        hidden_out[:, to : to + 256] = hidden
        total = total + nt(hidden, both[:, at + 128 : at + BLK])
    out[...] += total


def dense_backward_kernel(
    grad, rows, norm, hidden, slope, both, out, both_grad, norm_grad, low, normed_t, low_t, acc
):
    half, single = jnp.bfloat16, jnp.float32
    step = pl.program_id(0)

    @pl.when(step == 0)
    def _():
        xhat, _ = layer_normalize(rows[...])
        normed = (xhat * norm[0:1, :] + norm[1:2, :]).astype(half).astype(single)
        normed_t[...] = normed.T.astype(half)
        low[...] = grad[...].astype(half)
        low_t[...] = grad[...].T.astype(half)
        acc[...] = jnp.zeros_like(acc)

    total = jnp.zeros(acc.shape, single)
    for k in range(GROUP):
        at, to = k * BLK, k * 256
        hidden_grad = pltpu.roll(nn(low[...], both[:, at + 128 : at + BLK]), 192, 1)
        pre_grad = (hidden_grad * slope[:, to : to + 256]).astype(half)
        up = nn(normed_t[...], pre_grad)
        down = nn(low_t[...], hidden[:, to : to + 256])
        both_grad[:, at : at + 128] = up[:, 0:128].astype(half)
        both_grad[:, at + 128 : at + 256] = (up[:, 128:] + down[:, 0:128]).astype(half)
        both_grad[:, at + 256 : at + BLK] = down[:, 128:].astype(half)
        total = total + nt(pre_grad, both[:, at : at + 256])
    acc[...] += total

    @pl.when(step == pl.num_programs(0) - 1)
    def _():
        xhat, inverse = layer_normalize(rows[...])
        total = acc[...]
        norm_grad[0:1, :] = jnp.sum(total * xhat, axis=0, keepdims=True)
        norm_grad[1:2, :] = jnp.sum(total, axis=0, keepdims=True)
        out[...] = grad[...] + norm_backward_pass(total, xhat, inverse, norm[0:1, :])


def dense_forward(rows, norm, both):
    single, half = jnp.float32, jnp.bfloat16
    depth, wide = both.shape
    steps = wide // BLK
    shape = jax.ShapeDtypeStruct
    still = pl.BlockSpec((PADDED, depth), lambda i: (0, 0))
    moving = pl.BlockSpec((PADDED, GROUP * 256), lambda i: (0, i))
    return pl.pallas_call(
        dense_forward_kernel,
        grid=(steps // GROUP,),
        out_shape=[
            shape((PADDED, depth), single),
            shape((PADDED, steps * 256), half),
            shape((PADDED, steps * 256), single),
        ],
        in_specs=[
            still,
            pl.BlockSpec((2, depth), lambda i: (0, 0)),
            pl.BlockSpec((depth, GROUP * BLK), lambda i: (0, i)),
        ],
        out_specs=[still, moving, moving],
        scratch_shapes=[pltpu.VMEM((PADDED, depth), half)],
        compiler_params=pltpu.CompilerParams(vmem_limit_bytes=56 * 2**20),
    )(rows, norm, both)


def dense_backward(grad, rows, norm, hidden, slope, both):
    single, half = jnp.float32, jnp.bfloat16
    depth, wide = both.shape
    shape = jax.ShapeDtypeStruct
    still = pl.BlockSpec((PADDED, depth), lambda i: (0, 0))
    moving = pl.BlockSpec((PADDED, GROUP * 256), lambda i: (0, i))
    pair = pl.BlockSpec((2, depth), lambda i: (0, 0))
    block = pl.BlockSpec((depth, GROUP * BLK), lambda i: (0, i))
    return pl.pallas_call(
        dense_backward_kernel,
        grid=(wide // BLK // GROUP,),
        out_shape=[
            shape((PADDED, depth), single),
            shape((depth, wide), half),
            shape((2, depth), single),
        ],
        in_specs=[still, still, pair, moving, moving, block],
        out_specs=[still, block, pair],
        scratch_shapes=[
            pltpu.VMEM((PADDED, depth), half),
            pltpu.VMEM((depth, PADDED), half),
            pltpu.VMEM((depth, PADDED), half),
            pltpu.VMEM((PADDED, depth), single),
        ],
        compiler_params=pltpu.CompilerParams(vmem_limit_bytes=56 * 2**20),
    )(grad, rows, norm, hidden, slope, both)


def keys_bias():
    lane = lax.broadcasted_iota(jnp.int32, (PADDED, PADDED), 1)
    return jnp.where(lane < SEQ, 0.0, -1e30)


def of_head(value, h):
    lane = lax.broadcasted_iota(jnp.int32, value.shape, 1)
    mine = (lane < HEAD_DIM) if h == 0 else (lane >= HEAD_DIM)
    return jnp.where(mine, value, jnp.zeros_like(value))


def attention_forward_kernel(rows, norm, weights, out, mixed, context, lse):
    half, single = jnp.bfloat16, jnp.float32
    depth = rows.shape[1]
    xhat, _ = layer_normalize(rows[...])
    normed = (xhat * norm[0:1, :] + norm[1:2, :]).astype(half)
    mixed[:, 0:depth] = (nn(normed, weights[:, 0:depth]) * 0.125).astype(half)
    mixed[:, depth : 3 * depth] = nn(normed, weights[:, depth : 3 * depth]).astype(half)
    bias = keys_bias()
    lane = lax.broadcasted_iota(jnp.int32, (PADDED, 128), 1)
    totals = jnp.zeros((PADDED, 128), single)
    for pair in range(HEADS // 2):
        at = pair * 128
        query = mixed[:, at : at + 128]
        key = mixed[:, depth + at : depth + at + 128]
        value = mixed[:, 2 * depth + at : 2 * depth + at + 128]
        made = jnp.zeros((PADDED, 128), single)
        for h in range(2):
            scores = nt(of_head(query, h), key) + bias
            top = jnp.max(scores, axis=1, keepdims=True)
            total = top + jnp.log(jnp.sum(jnp.exp(scores - top), axis=1, keepdims=True))
            probs = jnp.exp(scores - total).astype(half)
            made = made + of_head(nn(probs, value), h)
            totals = jnp.where(lane == 2 * pair + h, total, totals)
        context[:, at : at + 128] = made.astype(half)
    lse[...] = totals
    out[...] = rows[...] + nn(context[...], weights[:, 3 * depth : 4 * depth])


def attention_backward_kernel(
    grad, rows, norm, weights, mixed, context, lse, kept_grads, out, norm_grad, both_grad, mixed_grad
):
    half, single = jnp.bfloat16, jnp.float32
    depth = rows.shape[1]
    xhat, inverse = layer_normalize(rows[...])
    normed_t = (xhat * norm[0:1, :] + norm[1:2, :]).astype(half).astype(single).T.astype(half)
    low = grad[...].astype(half)
    context_t = context[...].astype(single).T.astype(half)
    both_grad[:, 3 * depth : 4 * depth] = nn(context_t, low).astype(half)
    context_grad = nt(low, weights[:, 3 * depth : 4 * depth]).astype(half)
    bias = keys_bias()
    totals = lse[...]
    for pair in range(HEADS // 2):
        at = pair * 128
        query = mixed[:, at : at + 128]
        key = mixed[:, depth + at : depth + at + 128]
        value = mixed[:, 2 * depth + at : 2 * depth + at + 128]
        turn = context_grad[:, at : at + 128]
        zero = jnp.zeros((PADDED, 128), single)
        query_grad, key_grad, value_grad = zero, zero, zero
        for h in range(2):
            k = 2 * pair + h
            probs = jnp.exp(nt(of_head(query, h), key) + bias - totals[:, k : k + 1])
            value_grad = value_grad + of_head(tn(probs.astype(half), turn), h)
            prob_grad = nt(of_head(turn, h), value)
            inner = jnp.sum(probs * prob_grad, axis=1, keepdims=True)
            score_grad = (probs * (prob_grad - inner)).astype(half)
            query_grad = query_grad + of_head(nn(score_grad, key), h)
            key_grad = key_grad + of_head(tn(score_grad, query), h)
        mixed_grad[:, at : at + 128] = (query_grad * 0.125).astype(half)
        mixed_grad[:, depth + at : depth + at + 128] = key_grad.astype(half)
        mixed_grad[:, 2 * depth + at : 2 * depth + at + 128] = value_grad.astype(half)
    both_grad[:, 0 : 3 * depth] = nn(normed_t, mixed_grad[...]).astype(half)
    total = nt(mixed_grad[...], weights[:, 0 : 3 * depth])
    norm_grad[0:1, :] = jnp.sum(total * xhat, axis=0, keepdims=True)
    norm_grad[1:2, :] = jnp.sum(total, axis=0, keepdims=True)
    full = grad[...] + norm_backward_pass(total, xhat, inverse, norm[0:1, :])
    out[...] = full[0 : out.shape[0], :]


def whole_block(shape):
    return pl.BlockSpec(shape, lambda i: (0, 0))


def attention_forward(rows, norm, weights, which):
    half, single = jnp.bfloat16, jnp.float32
    count, depth = rows.shape
    shape = jax.ShapeDtypeStruct
    outs = [
        shape((count, depth), single),
        shape((count, 3 * depth), half),
        shape((count, depth), half),
        shape((count, 128), single),
    ]
    return pl.pallas_call(
        attention_forward_kernel,
        grid=(1,),
        out_shape=outs,
        in_specs=[
            whole_block(rows.shape),
            whole_block(norm.shape),
            pl.BlockSpec((depth, 4 * depth), lambda i: (0, which)),
        ],
        out_specs=[whole_block(o.shape) for o in outs],
        compiler_params=pltpu.CompilerParams(vmem_limit_bytes=48 * 2**20),
    )(rows, norm, weights)


def attention_backward(grad, rows, norm, weights, saved, which, filled, keep):
    half, single = jnp.bfloat16, jnp.float32
    count, depth = rows.shape
    mixed, context, lse = saved
    shape = jax.ShapeDtypeStruct
    block = pl.BlockSpec((depth, 4 * depth), lambda i: (0, which))
    operands = [grad, rows, norm, weights, mixed, context, lse]
    in_specs = [
        whole_block(grad.shape), whole_block(rows.shape), whole_block(norm.shape), block,
        whole_block(mixed.shape), whole_block(context.shape), whole_block(lse.shape),
    ]
    if filled is None:
        body_kernel = lambda *refs: attention_backward_kernel(*refs[:7], None, *refs[7:])
        aliases = {}
    else:
        body_kernel = attention_backward_kernel
        operands.append(filled)
        in_specs.append(pl.BlockSpec(memory_space=pl.ANY))
        aliases = {7: 2}
    return pl.pallas_call(
        body_kernel,
        grid=(1,),
        out_shape=[
            shape((keep, depth), single), shape((2, depth), single), shape(weights.shape, half)
        ],
        in_specs=in_specs,
        out_specs=[whole_block((keep, depth)), whole_block((2, depth)), block],
        scratch_shapes=[pltpu.VMEM((count, 3 * depth), half)],
        input_output_aliases=aliases,
        compiler_params=pltpu.CompilerParams(vmem_limit_bytes=56 * 2**20),
    )(*operands)


SLOTS = 32


def expert_kernel(
    sent, w_in, w_out, home, in_grad, out_grad,
    came, ret, wi, wo, slope, hidden, pre_grad, acc, rows_t, cot_t, stage_in, stage_out,
    loads, stores, s1, r1, s2, r2,
):
    half, single = jnp.bfloat16, jnp.float32
    dp, e, _, _, _, _ = place()
    parts = wi.shape[0]
    rows_count = 16 * SLOTS
    depth = wi.shape[1]

    def fetch(b, k):
        source, target = ((w_in, wi), (w_out, wo))[k]
        return pltpu.make_async_copy(source.at[b], target.at[b], loads.at[b, k])

    def begin(b, carry):
        fetch(b, 0).start()
        fetch(b, 1).start()
        return carry

    lax.fori_loop(0, parts, begin, 0)
    barrier = pltpu.get_barrier_semaphore()

    def greet(k, carry):
        pl.semaphore_signal(
            barrier, inc=1, device_id=(dp, lax.rem(e + k, 16)), device_id_type=MESH
        )
        return carry

    lax.fori_loop(1, 16, greet, 0)
    pl.semaphore_wait(barrier, 15)

    def route(source, target, which, k, send_sem, recv_sem):
        peer = lax.rem(e + k, 16)
        cut = pl.ds(which * SLOTS, SLOTS)
        return send(
            source.at[peer, cut],
            target.at[e, cut],
            send_sem.at[which, k],
            recv_sem.at[which, k],
            (dp, peer),
        )

    def depart(source, target, which, send_sem, recv_sem):
        def one(k, carry):
            route(source, target, which, k, send_sem, recv_sem).start()
            return carry

        lax.fori_loop(1, 16, one, 0)

    def arrive(source, target, which, send_sem, recv_sem):
        def one(k, carry):
            route(source, target, which, k, send_sem, recv_sem).wait()
            return carry

        lax.fori_loop(1, 16, one, 0)

    depart(sent, came, 0, s1, r1)
    depart(sent, came, 1, s1, r1)
    came[e] = sent[e]
    arrive(sent, came, 0, s1, r1)
    rows = came[:, 0:SLOTS, :].reshape(rows_count, depth)
    acc[...] = jnp.zeros_like(acc)

    def forward(b, carry):
        fetch(b, 0).wait()
        fetch(b, 1).wait()
        value, rise = gelu_pair(nn(rows, wi[b]))
        slope[b] = rise
        mid = value.astype(half)
        hidden[b] = mid
        acc[...] += nn(mid, wo[b])
        return carry

    lax.fori_loop(0, parts, forward, 0)
    ret[:, 0:SLOTS, :] = acc[...].astype(half).reshape(16, SLOTS, depth)
    depart(ret, home, 0, s2, r2)
    rows_t[...] = rows.T
    arrive(sent, came, 1, s1, r1)
    cot = came[:, SLOTS:, :].reshape(rows_count, depth)
    acc[...] = jnp.zeros_like(acc)

    def backward(b, carry):
        grad = (nt(cot, wo[b]) * slope[b]).astype(half)
        pre_grad[b] = grad
        acc[...] += nt(grad, wi[b])
        return carry

    lax.fori_loop(0, parts, backward, 0)
    ret[:, SLOTS:, :] = acc[...].astype(half).reshape(16, SLOTS, depth)
    depart(ret, home, 1, s2, r2)
    home[e] = ret[e]
    cot_t[...] = cot.T

    def store(b, k):
        source, target = ((stage_in, in_grad), (stage_out, out_grad))[k]
        return pltpu.make_async_copy(source.at[b], target.at[b], stores.at[b, k])

    def weigh(b, carry):
        stage_in[b] = nn(rows_t[...], pre_grad[b]).astype(half)
        store(b, 0).start()
        stage_out[b] = nn(cot_t[...], hidden[b]).astype(half)
        store(b, 1).start()
        return carry

    lax.fori_loop(0, parts, weigh, 0)

    def settle(b, carry):
        store(b, 0).wait()
        store(b, 1).wait()
        return carry

    lax.fori_loop(0, parts, settle, 0)
    arrive(ret, home, 0, s2, r2)
    arrive(ret, home, 1, s2, r2)


def expert_pass(sent, w_in, w_out):
    half, single = jnp.bfloat16, jnp.float32
    parts, depth, inner = w_in.shape
    count = 16 * SLOTS
    shape = jax.ShapeDtypeStruct
    vmem = pl.BlockSpec(memory_space=pltpu.VMEM)
    hbm = pl.BlockSpec(memory_space=pl.ANY)
    dma = pltpu.SemaphoreType.DMA
    return pl.pallas_call(
        expert_kernel,
        out_shape=[shape(sent.shape, half), shape(w_in.shape, half), shape(w_in.shape, half)],
        in_specs=[vmem, hbm, hbm],
        out_specs=[vmem, hbm, hbm],
        scratch_shapes=[
            pltpu.VMEM(sent.shape, half),
            pltpu.VMEM(sent.shape, half),
            pltpu.VMEM(w_in.shape, half),
            pltpu.VMEM(w_out.shape, half),
            pltpu.VMEM((parts, count, inner), single),
            pltpu.VMEM((parts, count, inner), half),
            pltpu.VMEM((parts, count, inner), half),
            pltpu.VMEM((count, depth), single),
            pltpu.VMEM((depth, count), half),
            pltpu.VMEM((depth, count), half),
            pltpu.VMEM(w_in.shape, half),
            pltpu.VMEM(w_in.shape, half),
            dma((parts, 2)), dma((parts, 2)),
            dma((2, 16)), dma((2, 16)), dma((2, 16)), dma((2, 16)),
        ],
        compiler_params=pltpu.CompilerParams(
            collective_id=2, has_side_effects=True, vmem_limit_bytes=56 * 2**20
        ),
    )(sent, w_in, w_out)


def adam_kernel(rates, turned, cuts, *refs):
    count = len(rates)
    params, states, grads = refs[:count], refs[count : 2 * count], refs[2 * count : 3 * count]
    outs, scratch = refs[3 * count : 6 * count], refs[6 * count :]
    near, sems = scratch[:-1], scratch[-1]
    order = sorted(range(count), key=lambda k: -params[k].size)
    first_scale, second_scale = 1.0 / (1.0 - beta_one**STEP), 1.0 / (1.0 - beta_two**STEP)

    def chunks(k):
        if params[k].ndim < 3:
            return [(0, None)]
        step = params[k].shape[1] // 3
        return [(n, pl.ds(n * step, step)) for n in range(3)]

    def cut(ref, which, part):
        if part is None:
            return ref
        return ref.at[:, :, part] if which == 1 else ref.at[:, part]

    def load(k, which, n, part):
        source = (params, states)[which][k]
        return pltpu.make_async_copy(
            cut(source, which, part), cut(near[3 * k + which], which, part), sems.at[0, k, which, n]
        )

    def store(k, which, n, part):
        held, kind = ((2, 0), (0, 0), (1, 1))[which]
        return pltpu.make_async_copy(
            cut(near[3 * k + held], kind, part),
            cut(outs[3 * k + which], kind, part),
            sems.at[1, k, which, n],
        )

    for k in order:
        for spot in chunks(k):
            load(k, 0, *spot).start()
            load(k, 1, *spot).start()
    for k in order:
        for n, part in chunks(k):
            how = cuts[k]
            rows = slice(None) if part is None else slice(part.start, part.start + part.size)
            if how is None and part is None:
                grad = grads[k][...]
            elif how is None and grads[k].shape == params[k].shape:
                grad = grads[k][:, rows].astype(jnp.float32)
            elif how is None:
                grad = grads[k][0, :, rows].astype(jnp.float32).T[None]
            elif how[0] == "rows":
                grad = grads[k][...].T[how[1] : how[2], :]
            else:
                grad = grads[k][:, how[1] : how[2]]
            held, param, state = near[3 * k + 2], near[3 * k], near[3 * k + 1]
            here = (Ellipsis,) if part is None else (slice(None), rows)
            held[here] = grad
            store(k, 0, n, part).start()
            load(k, 0, n, part).wait()
            load(k, 1, n, part).wait()
            rate, decay = rates[k]
            if turned[k]:
                lower, upper = (slice(None), 0), (slice(None), 1)
            elif part is None:
                lower, upper = (0,), (1,)
            else:
                lower, upper = (0, slice(None), rows), (1, slice(None), rows)
            first = beta_one * state[lower] + (1.0 - beta_one) * grad
            second = beta_two * state[upper] + (1.0 - beta_two) * grad * grad
            update = first * first_scale / (jnp.sqrt(second * second_scale) + adam_eps)
            param[here] = param[here] - rate * (update + decay * param[here])
            state[lower] = first
            state[upper] = second
            store(k, 1, n, part).start()
            store(k, 2, n, part).start()
    for k in order:
        for spot in chunks(k):
            for which in range(3):
                store(k, which, *spot).wait()


def adam_all(params, states, grads, rates, cuts):
    single = jnp.float32
    vmem = pl.BlockSpec(memory_space=pltpu.VMEM)
    hbm = pl.BlockSpec(memory_space=pl.ANY)
    shape = jax.ShapeDtypeStruct
    outs, near = [], []
    turned = [param.shape[0] == 6 for param in params]
    states = [s.swapaxes(0, 1) if t else s for s, t in zip(states, turned)]
    for param, state in zip(params, states):
        outs += [shape(param.shape, single), shape(param.shape, single), shape(state.shape, single)]
        near += [pltpu.VMEM(s.shape, single) for s in (param, state, param)]
    results = pl.pallas_call(
        functools.partial(adam_kernel, rates, turned, cuts),
        out_shape=outs,
        in_specs=[hbm] * (2 * len(params)) + [vmem] * len(params),
        out_specs=[hbm] * len(outs),
        scratch_shapes=[*near, pltpu.SemaphoreType.DMA((2, len(params), 3, 3))],
        compiler_params=pltpu.CompilerParams(vmem_limit_bytes=56 * 2**20),
    )(*params, *states, *grads)
    results = list(results)
    for k, flip in enumerate(turned):
        if flip:
            results[3 * k + 2] = results[3 * k + 2].swapaxes(0, 1)
    return results


def body(
    tokens,
    routes,
    cotangent,
    lead_norm_one,
    lead_norm_one_state,
    lead_mix,
    lead_mix_state,
    lead_project,
    lead_project_state,
    lead_norm_two,
    lead_norm_two_state,
    lead_up,
    lead_up_state,
    lead_down,
    lead_down_state,
    norm_first,
    norm_first_state,
    mix_weight,
    mix_state,
    project_weight,
    project_state,
    norm_second,
    norm_second_state,
    router_weight,
    router_state,
    expert_in,
    expert_in_state,
    expert_out,
    expert_out_state,
):
    half = jnp.bfloat16
    single = jnp.float32
    count, width = tokens.shape
    experts = router_weight.shape[1]
    planes = lax.axis_size("expert")
    slot_rows = 32
    small = jnp.concatenate(
        [lead_norm_one.T, lead_norm_two.T, norm_first.T, norm_second.T, router_weight], axis=1
    )
    small = jnp.pad(small, ((0, 0), (0, 128 - small.shape[1])))
    dense = jnp.concatenate([lead_up, lead_down.T], axis=1).astype(half)
    own_full, dense_full, small_full = gather_weights(
        lead_mix, lead_project, mix_weight, project_weight, small, dense
    )
    own_full = own_full.reshape(width, -1)
    dense_full = dense_full.reshape(width, -1)
    small_full = small_full.reshape(width, -1)
    in_full = lax.all_gather(expert_in[0].astype(half), "dp", axis=0)
    out_full = lax.all_gather(expert_out[0].astype(half), "dp", axis=0)
    norms = small_full[:, :8].T.astype(single)
    router_half = small_full[:, 8:24]
    extra = ((0, PADDED - count), (0, 0))
    first_rows = jnp.pad(tokens.astype(single), extra)
    after_a, *saved_a = attention_forward(first_rows, norms[0:2], own_full, 0)
    layer_one, up_hidden, up_slope = dense_forward(after_a, norms[2:4], dense_full)
    after_attn, *saved_one = attention_forward(layer_one, norms[4:6], own_full, 1)
    after_attn = after_attn[:count]
    xhat_two, inv_two = layer_normalize(after_attn)
    normed_two = (xhat_two * norms[6] + norms[7]).astype(half)
    logits = dot_nn(normed_two, router_half)
    ids = jnp.arange(experts, dtype=jnp.int32)
    picks = [(routes[:, k : k + 1] == ids[None, :]).astype(single) for k in range(2)]
    level = [jnp.sum(p * logits, axis=1, keepdims=True) for p in picks]
    gates = [
        1.0 / (1.0 + jnp.exp(level[1] - level[0])),
        1.0 / (1.0 + jnp.exp(level[0] - level[1])),
    ]
    named = jnp.concatenate(picks, axis=0)
    at = jnp.arange(2 * count, dtype=jnp.int32)
    before = (at[:, None] > at[None, :]).astype(half)
    place = jnp.sum(dot_nn(before, named.astype(half)) * named, axis=1).astype(jnp.int32)
    target = jnp.concatenate([routes[:, 0], routes[:, 1]]) * slot_rows + place
    slots = jnp.arange(experts * slot_rows, dtype=jnp.int32)
    table = (target[:, None] == slots[None, :]).astype(half)
    upstream = cotangent.astype(single)
    row_cot = jnp.concatenate([(g * upstream).astype(half) for g in gates], axis=0)
    sent = jnp.concatenate(
        [
            dot_tn(table[:count] + table[count:], normed_two)
            .astype(half)
            .reshape(experts, slot_rows, width),
            dot_tn(table, row_cot).astype(half).reshape(experts, slot_rows, width),
        ],
        axis=1,
    )
    back, in_part, out_part = expert_pass(sent, in_full, out_full)
    in_sum = lax.psum_scatter(in_part, "dp", scatter_dimension=0, tiled=True)
    out_sum = lax.psum_scatter(out_part, "dp", scatter_dimension=0, tiled=True)
    combined = back[:, :slot_rows].reshape(-1, width)
    returned = back[:, slot_rows:].reshape(-1, width)
    outputs = [dot_nn(table[:count], combined), dot_nn(table[count:], combined)]
    block_out = (after_attn + gates[0] * outputs[0] + gates[1] * outputs[1]).astype(half)
    gate_diff = jnp.sum(upstream * (outputs[0] - outputs[1]), axis=1, keepdims=True)
    logit_grad = (gates[0] * gates[1] * gate_diff * (picks[0] - picks[1])).astype(half)
    router_grad = dot_tn(normed_two, logit_grad)
    normed_two_grad = dot_nn(table[:count] + table[count:], returned) + dot_nt(
        logit_grad, router_half
    )
    norm_two_grad = jnp.stack(
        [jnp.sum(normed_two_grad * xhat_two, axis=0), jnp.sum(normed_two_grad, axis=0)]
    )
    attn_grad = upstream + norm_backward_pass(normed_two_grad, xhat_two, inv_two, norms[6])
    layer_one_grad, norm_one_grad, own_grad = attention_backward(
        jnp.pad(attn_grad, extra), layer_one, norms[4:6], own_full, saved_one, 1, None, PADDED
    )
    after_a_grad, dense_grad, lead_two_grad = dense_backward(
        layer_one_grad, after_a, norms[2:4], up_hidden, up_slope, dense_full
    )
    token_input_grad, lead_one_grad, own_grad = attention_backward(
        after_a_grad, first_rows, norms[0:2], own_full, saved_a, 0, own_grad, count
    )
    small_grad = jnp.concatenate(
        [
            jnp.concatenate([lead_one_grad, lead_two_grad, norm_one_grad, norm_two_grad], axis=0).T,
            router_grad,
        ],
        axis=1,
    )
    small_grad = jnp.pad(small_grad, ((0, 0), (0, 128 - small_grad.shape[1]))).astype(half)
    lead_mix_sum, lead_project_sum, mix_sum, project_sum, small_sum, dense_sum = scatter_grads(
        own_grad.reshape(4, 2, ROWS, -1),
        dense_grad.reshape(4, 2, ROWS, -1),
        small_grad.reshape(4, 2, ROWS, -1),
    )
    norm, matrix = (norm_rate, 0.0), (matrix_rate, decay_rate)
    table = (
        (lead_norm_one, lead_norm_one_state, small_sum, norm, ("rows", 0, 2)),
        (lead_mix, lead_mix_state, lead_mix_sum, matrix, None),
        (lead_project, lead_project_state, lead_project_sum, matrix, None),
        (lead_norm_two, lead_norm_two_state, small_sum, norm, ("rows", 2, 4)),
        (lead_up, lead_up_state, dense_sum, matrix, ("cols", 0, 192)),
        (lead_down, lead_down_state, dense_sum, matrix, ("rows", 192, 384)),
        (norm_first, norm_first_state, small_sum, norm, ("rows", 4, 6)),
        (mix_weight, mix_state, mix_sum, matrix, None),
        (project_weight, project_state, project_sum, matrix, None),
        (norm_second, norm_second_state, small_sum, norm, ("rows", 6, 8)),
        (router_weight, router_state, small_sum, matrix, ("cols", 8, 24)),
        (expert_in, expert_in_state, in_sum, matrix, None),
        (expert_out, expert_out_state, out_sum, matrix, None),
    )
    params, states, grads, rates, cuts = zip(*table)
    return (block_out, token_input_grad, *adam_all(params, states, grads, rates, cuts))


def solution(mesh):
    placed = (
        P(("dp", "expert"), None),
        P(("dp", "expert"), None),
        P(("dp", "expert"), None),
        P(None, ("dp", "expert")),
        P(None, None, ("dp", "expert")),
        P(("dp", "expert"), None),
        P(None, ("dp", "expert"), None),
        P(("dp", "expert"), None),
        P(None, ("dp", "expert"), None),
        P(None, ("dp", "expert")),
        P(None, None, ("dp", "expert")),
        P("dp", "expert"),
        P(None, "dp", "expert"),
        P("expert", "dp"),
        P(None, "expert", "dp"),
        P(None, ("dp", "expert")),
        P(None, None, ("dp", "expert")),
        P(("dp", "expert"), None),
        P(None, ("dp", "expert"), None),
        P(("dp", "expert"), None),
        P(None, ("dp", "expert"), None),
        P(None, ("dp", "expert")),
        P(None, None, ("dp", "expert")),
        P(("dp", "expert"), None),
        P(None, ("dp", "expert"), None),
        P("expert", None, "dp"),
        P(None, "expert", None, "dp"),
        P("expert", "dp", None),
        P(None, "expert", "dp", None),
    )
    return jax.shard_map(
        body,
        mesh=mesh,
        in_specs=placed,
        out_specs=(
            P(("dp", "expert"), None),
            P(("dp", "expert"), None),
            P(None, ("dp", "expert")),
            P(None, ("dp", "expert")),
            P(None, None, ("dp", "expert")),
            P(("dp", "expert"), None),
            P(("dp", "expert"), None),
            P(None, ("dp", "expert"), None),
            P(("dp", "expert"), None),
            P(("dp", "expert"), None),
            P(None, ("dp", "expert"), None),
            P(None, ("dp", "expert")),
            P(None, ("dp", "expert")),
            P(None, None, ("dp", "expert")),
            P("dp", "expert"),
            P("dp", "expert"),
            P(None, "dp", "expert"),
            P("expert", "dp"),
            P("expert", "dp"),
            P(None, "expert", "dp"),
            P(None, ("dp", "expert")),
            P(None, ("dp", "expert")),
            P(None, None, ("dp", "expert")),
            P(("dp", "expert"), None),
            P(("dp", "expert"), None),
            P(None, ("dp", "expert"), None),
            P(("dp", "expert"), None),
            P(("dp", "expert"), None),
            P(None, ("dp", "expert"), None),
            P(None, ("dp", "expert")),
            P(None, ("dp", "expert")),
            P(None, None, ("dp", "expert")),
            P(("dp", "expert"), None),
            P(("dp", "expert"), None),
            P(None, ("dp", "expert"), None),
            P("expert", None, "dp"),
            P("expert", None, "dp"),
            P(None, "expert", None, "dp"),
            P("expert", "dp", None),
            P("expert", "dp", None),
            P(None, "expert", "dp", None),
        ),
        check_vma=False,
    )
```
